256 devices in a mesh: ctx: 16 (over z, core), head: 16 (over y, x).
Axes of the slice: x: 4, y: 4, z: 8, core: 2. Of those that a mesh axis runs over, the one named last changes fastest.
Arguments:
- inputs: bfloat16 [16384, 8192], P('ctx', 'head'), may hold values from -6 to 6
- upstream: bfloat16 [16384, 8192], P('ctx', 'head'), may hold values from -1.1953125 to 1.1953125
- step_size: float32 [16384, 128], P('ctx', 'head'), may hold values from 0 to 0.5, as said below
- decay_rate: float32 [128], P('head'), may hold values from 0 to 0.16, as said below
- write_proj: bfloat16 [16384, 1024], P('ctx'), may hold values from -2.390625 to 2.390625
- read_proj: bfloat16 [16384, 1024], P('ctx'), may hold values from -2.390625 to 2.390625
- init_state: float32 [128, 64, 128], P('head'), may hold values from -6 to 6
- skip_gain: float32 [128], P('head'), may hold values from 0.5 to 2
Outputs:
- grad_inputs: bfloat16 [16384, 8192], P(('ctx', 'head'))
- grad_write: bfloat16 [16384, 1024], P(('ctx', 'head'))
- grad_read: bfloat16 [16384, 1024], P(('ctx', 'head'))
The draws below stay inside these ranges and needn't reach their ends.
Inputs may be any that keep to these rules, and one draw needn't show every extreme that they name: `step_size`: positive step sizes. `decay_rate`: positive decay rates.
All inputs are finite; a program needn't handle non-finite values.
Results may differ from the reference program's by a relative error of at most 0.0024.
Values may be sent and summed in bfloat16 or wider, within the bound.
No kernel may reach another device: no remote copies, remote signals or barrier semaphores. Data moves between devices by JAX's collectives and lax.ppermute only.
A program may use at most 64 MiB of HBM per device.

```python
import jax
import jax.numpy as jnp
from jax import lax

HEADS = 128
HEAD_SIZE = 64
STATE = 128
GROUPS = 8
BLOCK = 256
TOKENS = 16384
N_HEAD = 16


def slow_heads(key, share):
    return jax.random.uniform(jax.random.fold_in(key, 77), (HEADS,), jnp.float32) < share


def draw_decay_rate(key, part):
    share = 0.5
    slow = slow_heads(key, share)
    key = jax.random.fold_in(key, 1)
    first, second = jax.random.split(key)
    fast = jnp.exp(jax.random.uniform(first, (HEADS,), jnp.float32, jnp.log(0.06), jnp.log(0.16)))
    drawn = jnp.exp(jax.random.uniform(second, (HEADS,), jnp.float32, jnp.log(0.45), jnp.log(1.8)))
    drawn = drawn / jnp.sqrt(TOKENS * 1.0)
    return jnp.where(slow, drawn, fast).astype(jnp.float32)


def draw_step_size(key, part):
    share = 0.5
    slow = slow_heads(key, share)
    key = jax.random.fold_in(key, 2)
    spread = jnp.exp(jax.random.uniform(key, (TOKENS, HEADS), jnp.float32, jnp.log(0.5), jnp.log(2.0)))
    scale = jnp.where(slow, 1.0 / jnp.sqrt(TOKENS * 1.0), 0.25)
    return (spread * scale[None, :]).astype(jnp.float32)


def block_scale(rng, dims, pieces, least, top_value):
    factor_of, own = 1.0, jax.random.fold_in(rng, 6)
    for axis_at, parts in pieces:
        heights = jnp.exp(jax.random.uniform(jax.random.fold_in(own, axis_at), (parts,), jnp.float32, least / len(pieces), top_value / len(pieces)))
        factor_of = factor_of * jnp.repeat(heights, dims[axis_at] // parts).reshape([-1 if axis == axis_at else 1 for axis in range(len(dims))])
    return factor_of


def scatter_about(rng, extent, width, limit, pieces=(), held_as=jnp.bfloat16):
    drawn = width * jax.random.normal(rng, extent, jnp.float32)
    if pieces:
        drawn = drawn * block_scale(rng, extent, pieces, -0.22, 0.18)
    return jnp.clip(drawn, -limit, limit).astype(held_as)


def setup_inputs(seed: int = 0) -> dict:
    keys = jax.random.split(jax.random.key(seed), 9)
    return {
        "inputs": scatter_about(keys[0], (TOKENS, HEADS * HEAD_SIZE), 1.0, 6.0, ((0, 16), (1, 16))),
        "upstream": scatter_about(keys[1], (TOKENS, HEADS * HEAD_SIZE), 0.2, 1.1953125, ((0, 16), (1, 16))),
        "step_size": draw_step_size(jax.random.fold_in(keys[8], 71), 0),
        "decay_rate": draw_decay_rate(jax.random.fold_in(keys[8], 71), 0),
        "write_proj": scatter_about(keys[4], (TOKENS, GROUPS * STATE), 0.4, 2.390625, ((0, 16),)),
        "read_proj": scatter_about(keys[5], (TOKENS, GROUPS * STATE), 0.4, 2.390625, ((0, 16),)),
        "init_state": scatter_about(keys[6], (HEADS, HEAD_SIZE, STATE), 1.0, 6.0, ((0, 16),), jnp.float32),
        "skip_gain": jnp.clip(0.5 + 1.5 * jax.random.uniform(keys[7], (HEADS,), jnp.float32) ** block_scale(keys[7], (HEADS,), ((0, 16),), -0.2, 0.2), 0.5, 2.0),
    }


highest = lax.Precision.HIGHEST


def decay_matrix(cum_log):
    length = cum_log.shape[0]
    lower = (jnp.arange(length)[:, None] >= jnp.arange(length)[None, :])[None, :, :]
    spread = cum_log.T[:, :, None] - cum_log.T[:, None, :]
    return jnp.where(lower, jnp.exp(jnp.where(lower, spread, 0.0)), 0.0)


def block_sums(inputs, upstream, steps, writes, reads, cum_log):
    last_log = cum_log[-1]
    weight_in = jnp.exp(last_log[None, :] - cum_log) * steps
    weight_back = jnp.exp(cum_log)
    into = jnp.einsum('thp,thn->hpn', weight_in[:, :, None] * inputs, writes, precision=highest)
    back = jnp.einsum('thp,thn->hpn', weight_back[:, :, None] * upstream, reads, precision=highest)
    return into, back


def expand_groups(writes_raw, reads_raw, repeat):
    dots = jnp.einsum('tgn,ugn->gtu', writes_raw, reads_raw, preferred_element_type=jnp.float32)
    return (jnp.repeat(writes_raw.astype(jnp.float32), repeat, axis=1),
            jnp.repeat(reads_raw.astype(jnp.float32), repeat, axis=1),
            jnp.repeat(dots, repeat, axis=0))


def block_grads(inputs, upstream, products, steps, writes, reads, pair_dots, cum_log, skip, state_in, adjoint_out):
    decays = decay_matrix(cum_log)
    last_log = cum_log[-1]
    kernel = products * decays
    weighted = kernel * steps.T[:, None, :]
    grad_read = jnp.exp(cum_log)[:, :, None] * jnp.einsum('thp,hpn->thn', upstream, state_in, precision=highest)
    grad_read = grad_read + jnp.einsum('hts,shn->thn', weighted, writes, precision=highest)
    remain = jnp.exp(last_log[None, :] - cum_log)[:, :, None]
    coupled = pair_dots * jnp.swapaxes(decays, 1, 2)
    through = jnp.einsum('htu,uhp->thp', coupled, upstream, precision=highest)
    through = through + remain * jnp.einsum('hpn,thn->thp', adjoint_out, writes, precision=highest)
    grad_input = steps[:, :, None] * through + skip[None, :, None] * upstream
    flipped = jnp.swapaxes(kernel, 1, 2)
    grad_write = jnp.einsum('htu,uhn->thn', flipped, reads, precision=highest)
    grad_write = grad_write + remain * jnp.einsum('thp,hpn->thn', inputs, adjoint_out, precision=highest)
    return grad_input, steps[:, :, None] * grad_write, grad_read


def group_total(grad_heads, sources, within):
    length = grad_heads.shape[0]
    partial_value = jnp.sum(grad_heads.reshape(length, GROUPS, sources, within, STATE), axis=3)
    partial_value = lax.optimization_barrier(partial_value.astype(jnp.bfloat16))
    summed = jnp.sum(partial_value.astype(jnp.float32), axis=2)
    return summed.astype(jnp.bfloat16).reshape(length, GROUPS * STATE)


def reference(inputs, upstream, step_size, decay_rate, write_proj, read_proj, init_state, skip_gain):
    per_group = HEADS // GROUPS
    heads_dev = HEADS // N_HEAD
    within = min(heads_dev, per_group)
    sources = per_group // within
    blocks = TOKENS // BLOCK
    shaped = (
        inputs.reshape(blocks, BLOCK, HEADS, HEAD_SIZE),
        upstream.reshape(blocks, BLOCK, HEADS, HEAD_SIZE),
        step_size.reshape(blocks, BLOCK, HEADS),
        write_proj.reshape(blocks, BLOCK, GROUPS, STATE),
        read_proj.reshape(blocks, BLOCK, GROUPS, STATE),
    )

    def unpack(raw):
        ins, ups, steps, wr_grp, rd_grp = raw
        cum_log = jnp.cumsum(-steps * decay_rate[None, :], axis=0)
        return ins.astype(jnp.float32), ups.astype(jnp.float32), steps, wr_grp.astype(jnp.float32), rd_grp.astype(jnp.float32), cum_log

    def forward_step(state, raw):
        ins, ups, steps, wr_grp, rd_grp, cum_log = unpack(raw)
        writes = jnp.repeat(wr_grp, per_group, axis=1)
        reads = jnp.repeat(rd_grp, per_group, axis=1)
        into, _ = block_sums(ins, ups, steps, writes, reads, cum_log)
        return jnp.exp(cum_log[-1])[:, None, None] * state + into, state

    _, states = lax.scan(forward_step, init_state, shaped)

    def backward_step(adjoint, pack):
        raw, state_in = pack
        ins, ups, steps, wr_grp, rd_grp, cum_log = unpack(raw)
        writes, reads, dots = expand_groups(raw[3], raw[4], per_group)
        products = jnp.einsum('thp,shp->hts', raw[1], raw[0], preferred_element_type=jnp.float32)
        _, back = block_sums(ins, ups, steps, writes, reads, cum_log)
        grad_input, grad_write, grad_read = block_grads(ins, ups, products, steps, writes, reads, dots, cum_log, skip_gain, state_in, adjoint)
        rows_input = grad_input.reshape(BLOCK, HEADS * HEAD_SIZE).astype(jnp.bfloat16)
        rows_write = group_total(grad_write, sources, within)
        rows_read = group_total(grad_read, sources, within)
        following = jnp.exp(cum_log[-1])[:, None, None] * adjoint + back
        return following, (rows_input, rows_write, rows_read)

    _, outcome = lax.scan(backward_step, jnp.zeros_like(init_state), (shaped, states), reverse=True)
    return (outcome[0].reshape(TOKENS, HEADS * HEAD_SIZE),
            outcome[1].reshape(TOKENS, GROUPS * STATE),
            outcome[2].reshape(TOKENS, GROUPS * STATE))
```

```python
import jax
import jax.numpy as jnp
from jax import lax
from jax.experimental import pallas as pl
from jax.experimental.pallas import tpu as pltpu
from jax.sharding import PartitionSpec as P

HEADS = 128
HEAD_SIZE = 64
STATE = 128
GROUPS = 8
TOKENS_DEV = 1024
HEADS_DEV = 8
FEATS = HEADS_DEV * HEAD_SIZE
CHUNK = 256
CHUNKS = TOKENS_DEV // CHUNK
CHIPS = 8
FAR = CHIPS // 2

f32 = jnp.float32
bf16 = jnp.bfloat16
VMEM_LIMIT = 40 * 1024 * 1024


def nn(a, b):
    return lax.dot_general(a, b, (((1,), (0,)), ((), ())), preferred_element_type=f32)


def nt(a, b):
    return lax.dot_general(a, b, (((1,), (1,)), ((), ())), preferred_element_type=f32)


def tn(a, b):
    return lax.dot_general(a, b, (((0,), (0,)), ((), ())), preferred_element_type=f32)


def halves(x):
    high = x.astype(bf16)
    return high, (x - high.astype(f32)).astype(bf16)


def head_columns():
    row = lax.broadcasted_iota(jnp.int32, (3 * HEADS_DEV, FEATS), 0) % HEADS_DEV
    col = lax.broadcasted_iota(jnp.int32, (3 * HEADS_DEV, FEATS), 1) // HEAD_SIZE
    return jnp.where(row == col, 1.0, 0.0).astype(bf16)


def spread(per_head, columns):
    high = per_head.astype(bf16).astype(f32)
    rest = per_head - high
    mid = rest.astype(bf16).astype(f32)
    low = rest - mid
    return tn(jnp.concatenate([high, mid, low], axis=0).astype(bf16), columns)


def head_vector(ref):
    row = lax.broadcasted_iota(jnp.int32, (HEADS_DEV, STATE), 0)
    out = jnp.zeros((HEADS_DEV, STATE), f32)
    for h in range(HEADS_DEV):
        out = jnp.where(row == h, ref[h], out)
    return out


def cumulate(x):
    lane = lax.broadcasted_iota(jnp.int32, x.shape, 1)
    hop = 1
    while hop < x.shape[1]:
        x = x + jnp.where(lane >= hop, pltpu.roll(x, hop, 1), 0.0)
        hop *= 2
    return x


def rows_of(i):
    return pl.ds(i * CHUNK, CHUNK)


def sums_kernel(
    u_hbm, dy_hbm, w_hbm, r_hbm, step_ref, rate_ref,
    out_ref, xdh_ref, xdl_ref, xuh_ref, xul_ref, dy_ref, w_ref, r_ref, bt_ref,
    u_ref, sems,
):
    column = pl.multiple_of(lax.axis_index("head") // 2 * STATE, STATE)
    copies = []
    for i in range(CHUNKS):
        rows = rows_of(i)
        group = [
            pltpu.make_async_copy(u_hbm.at[rows, :], u_ref.at[rows, :], sems.at[i, 0]),
            pltpu.make_async_copy(dy_hbm.at[rows, :], dy_ref.at[rows, :], sems.at[i, 1]),
            pltpu.make_async_copy(w_hbm.at[rows, pl.ds(column, STATE)], w_ref.at[rows, :], sems.at[i, 2]),
            pltpu.make_async_copy(r_hbm.at[rows, pl.ds(column, STATE)], r_ref.at[rows, :], sems.at[i, 3]),
        ]
        for copy in group:
            copy.start()
        copies.append(group)
    columns = head_columns()
    steps = step_ref[...]
    rate = head_vector(rate_ref)[:, :1]
    cum = cumulate(-steps * rate)
    last = cum[:, TOKENS_DEV - 1 :]
    middle = 0.5 * last
    ahead = jnp.exp(cum - middle)
    behind = jnp.exp(middle - cum) * steps
    bt_ref[...] = behind
    wide = lambda x: spread(jnp.broadcast_to(x, (HEADS_DEV, STATE)), columns)
    half = wide(jnp.exp(middle))
    acc_w = jnp.zeros((STATE, FEATS), f32)
    acc_r = jnp.zeros((STATE, FEATS), f32)
    for i in range(CHUNKS):
        rows = rows_of(i)
        for copy in copies[i]:
            copy.wait()
        high, low = halves(spread(behind[:, i * CHUNK : (i + 1) * CHUNK], columns) * u_ref[rows, :].astype(f32))
        xuh_ref[rows, :] = high
        xul_ref[rows, :] = low
        writes = w_ref[rows, :]
        acc_w = acc_w + tn(writes, high) + tn(writes, low)
        high, low = halves(spread(ahead[:, i * CHUNK : (i + 1) * CHUNK], columns) * dy_ref[rows, :].astype(f32))
        xdh_ref[rows, :] = high
        xdl_ref[rows, :] = low
        reads = r_ref[rows, :]
        acc_r = acc_r + tn(reads, high) + tn(reads, low)
    out_ref[pl.ds(0, STATE), :] = half * acc_w
    out_ref[pl.ds(STATE, STATE), :] = half * acc_r
    out_ref[pl.ds(2 * STATE, 8), :] = wide(last)[:8, :]


def message_kernel(own_ref, other_ref, a_ref, b_ref, c_ref, far_ref, w_ref, r_ref):
    place = lax.axis_index("ctx")
    chip, core = place // 2, place % 2
    own_log = own_ref[pl.ds(2 * STATE, 1), :]
    other_log = other_ref[pl.ds(2 * STATE, 1), :]
    own_decay = jnp.exp(own_log)
    other_decay = jnp.exp(other_log)
    first = core == 0
    one = jnp.ones_like(own_decay)
    w_ref[...] = (
        jnp.where(first, other_decay, one) * own_ref[pl.ds(0, STATE), :]
        + jnp.where(first, one, own_decay) * other_ref[pl.ds(0, STATE), :]
    )
    r_ref[...] = (
        jnp.where(first, one, other_decay) * own_ref[pl.ds(STATE, STATE), :]
        + jnp.where(first, own_decay, one) * other_ref[pl.ds(STATE, STATE), :]
    )
    logs = jnp.broadcast_to(own_log + other_log, (8, FEATS))
    for hop, ref in ((1, a_ref), (2, b_ref), (3, c_ref)):
        to_later = jnp.where(first, chip + hop < CHIPS, chip - hop < 0)

        @pl.when(to_later)
        def _():
            ref[pl.ds(0, STATE), :] = w_ref[...]

        @pl.when(jnp.logical_not(to_later))
        def _():
            ref[pl.ds(0, STATE), :] = r_ref[...]

        ref[pl.ds(STATE, 8), :] = logs
    half = FEATS // 2
    later = chip < FAR
    for part in range(2):
        cols = pl.ds(part * half, half)

        @pl.when(jnp.logical_and(later, core == part))
        def _():
            far_ref[pl.ds(0, STATE), :] = w_ref[:, cols]

        @pl.when(jnp.logical_and(jnp.logical_not(later), core == part))
        def _():
            far_ref[pl.ds(0, STATE), :] = r_ref[:, cols]

        @pl.when(core == part)
        def _():
            far_ref[pl.ds(STATE, 8), :] = logs[:, part * half : (part + 1) * half]


def local_kernel(
    xdh_ref, xdl_ref, xuh_ref, xul_ref, dy_ref, w_ref, r_ref, bt_ref, skip_ref, init_ref,
    gi_ref, back_ref, pw_ref, pr_ref, init_t_ref,
):
    columns = head_columns()
    skip = spread(head_vector(skip_ref), columns)[:1, :]
    init_t_ref[...] = init_ref[...].reshape(FEATS, STATE).T
    row = lax.broadcasted_iota(jnp.int32, (CHUNK, CHUNK), 0)
    col = lax.broadcasted_iota(jnp.int32, (CHUNK, CHUNK), 1)
    keep = col >= row
    for j in range(CHUNKS):
        to = rows_of(j)
        writes = w_ref[to, :]
        uh, ul = xuh_ref[to, :], xul_ref[to, :]
        acc_gi = jnp.zeros((CHUNK, FEATS), f32)
        acc_pw = jnp.zeros((CHUNK, STATE), f32)
        for i in range(j, CHUNKS):
            at = rows_of(i)
            dh, dl = xdh_ref[at, :], xdl_ref[at, :]
            reads = r_ref[at, :]
            pairs = nt(uh, dh) + nt(uh, dl) + nt(ul, dh)
            dots = nt(writes, reads)
            if i == j:
                pairs = jnp.where(keep, pairs, 0.0)
                dots = jnp.where(keep, dots, 0.0)
            ph, plow = halves(pairs)
            gh, gl = halves(dots)
            acc_pw = acc_pw + nn(ph, reads) + nn(plow, reads)
            part = tn(ph, writes) + tn(plow, writes)
            pr_ref[at, :] = part if j == 0 else pr_ref[at, :] + part
            acc_gi = acc_gi + nn(gh, dh) + nn(gh, dl) + nn(gl, dh)
        back = spread(bt_ref[:, j * CHUNK : (j + 1) * CHUNK], columns)
        back_ref[to, :] = back
        gi_ref[to, :] = back * acc_gi + skip * dy_ref[to, :].astype(f32)
        pw_ref[to, :] = acc_pw


def finish_kernel(
    own_ref, other_ref, a_ref, b_ref, c_ref, far_ref, oa_ref, ob_ref, oc_ref, ofar_ref,
    xdh_ref, xdl_ref, xuh_ref, xul_ref, w_ref, gi_ref, back_ref, pw_ref, pr_ref, init_t_ref,
    rows_ref, s_ref, t_ref,
):
    place = lax.axis_index("ctx")
    chip, core = place // 2, place % 2
    first = core == 0

    def pick(rows, hop):
        mine = (a_ref, b_ref, c_ref)[hop - 1][rows, :]
        theirs = (oa_ref, ob_ref, oc_ref)[hop - 1][rows, :]
        return jnp.where(first, mine, theirs), jnp.where(first, theirs, mine)

    def pick_far(rows):
        mine, theirs = far_ref[rows, :], ofar_ref[rows, :]
        return jnp.concatenate(
            [jnp.where(first, mine, theirs), jnp.where(first, theirs, mine)], axis=1
        )

    def distant(rows):
        below, above = {}, {}
        for hop in range(1, FAR):
            low, high = pick(rows, hop)
            below[hop], above[CHIPS - hop] = low, low
            above[hop], below[CHIPS - hop] = high, high
        middle = pick_far(rows)
        below[FAR], above[FAR] = middle, middle
        return below, above

    below_log, above_log = distant(pl.ds(STATE, 1))
    weights_s, weights_a = {}, {}
    total = jnp.zeros((1, FEATS), f32)
    for hop in range(1, CHIPS):
        valid = chip - hop >= 0
        weights_s[hop] = jnp.where(valid, jnp.exp(total), 0.0)
        total = total + jnp.where(valid, below_log[hop], 0.0)
    weight_init = jnp.exp(total)
    total = jnp.zeros((1, FEATS), f32)
    for hop in range(1, CHIPS):
        valid = chip + hop < CHIPS
        weights_a[hop] = jnp.where(valid, jnp.exp(total), 0.0)
        total = total + jnp.where(valid, above_log[hop], 0.0)

    own_log = own_ref[pl.ds(2 * STATE, 1), :]
    other_decay = jnp.exp(other_ref[pl.ds(2 * STATE, 1), :])
    half = jnp.exp(0.5 * own_log)
    for at in range(0, STATE, 32):
        rows = pl.ds(at, 32)
        below, above = distant(rows)
        state = weight_init * init_t_ref[rows, :]
        adjoint = jnp.zeros((32, FEATS), f32)
        for hop in range(1, CHIPS):
            state = state + weights_s[hop] * below[hop]
            adjoint = adjoint + weights_a[hop] * above[hop]
        state = jnp.where(first, state, other_ref[rows, :] + other_decay * state)
        adjoint = jnp.where(
            first, other_ref[pl.ds(STATE + at, 32), :] + other_decay * adjoint, adjoint
        )
        high, low = halves(half * state)
        s_ref[rows, :] = high
        s_ref[pl.ds(STATE + at, 32), :] = low
        high, low = halves(half * adjoint)
        t_ref[rows, :] = high
        t_ref[pl.ds(STATE + at, 32), :] = low

    for i in range(CHUNKS):
        rows = rows_of(i)
        reads = nt(xdh_ref[rows, :], s_ref[...])
        reads = reads[:, :STATE] + reads[:, STATE:] + nt(xdl_ref[rows, :], s_ref[pl.ds(0, STATE), :])
        writes = nt(xuh_ref[rows, :], t_ref[...])
        writes = writes[:, :STATE] + writes[:, STATE:] + nt(xul_ref[rows, :], t_ref[pl.ds(0, STATE), :])
        vectors = w_ref[rows, :]
        through = nn(jnp.concatenate([vectors, vectors], axis=1), t_ref[...])
        rows_ref[rows, pl.ds(0, FEATS)] = (gi_ref[rows, :] + back_ref[rows, :] * through).astype(bf16)
        rows_ref[rows, pl.ds(FEATS, STATE)] = (pw_ref[rows, :] + writes).astype(bf16)
        rows_ref[rows, pl.ds(FEATS + STATE, STATE)] = (pr_ref[rows, :] + reads).astype(bf16)


def arrange_kernel(in_ref, gi_ref, gw_ref, gr_ref):
    share = gi_ref.shape[0]
    peers = in_ref.shape[0] // share
    for j in range(peers):
        gi_ref[:, pl.ds(j * FEATS, FEATS)] = in_ref[pl.ds(j * share, share), pl.ds(0, FEATS)]
    for g in range(GROUPS):
        one, two = pl.ds(2 * g * share, share), pl.ds((2 * g + 1) * share, share)
        for ref, at in ((gw_ref, FEATS), (gr_ref, FEATS + STATE)):
            cols = pl.ds(at, STATE)
            ref[:, pl.ds(g * STATE, STATE)] = (
                in_ref[one, cols].astype(f32) + in_ref[two, cols].astype(f32)
            ).astype(bf16)


def call(body, outs, ins, scratch=(), flops=0):
    return pl.pallas_call(
        body,
        out_shape=outs,
        in_specs=ins,
        scratch_shapes=scratch,
        compiler_params=pltpu.CompilerParams(vmem_limit_bytes=VMEM_LIMIT),
        cost_estimate=pl.CostEstimate(flops=flops, bytes_accessed=1 << 20, transcendentals=0),
    )


IN_HBM = pl.BlockSpec(memory_space=pl.ANY)
IN_VMEM = pl.BlockSpec(memory_space=pltpu.VMEM)
IN_SMEM = pl.BlockSpec(memory_space=pltpu.SMEM)


def per_device(inputs, upstream, step_size, decay_rate, write_proj, read_proj, init_state, skip_gain):
    length = TOKENS_DEV
    wide = pltpu.VMEM((length, FEATS), bf16)
    wide32 = pltpu.VMEM((length, FEATS), f32)
    thin = pltpu.VMEM((length, STATE), bf16)
    thin32 = pltpu.VMEM((length, STATE), f32)
    own, xdh, xdl, xuh, xul, dy, w, r, bt = call(
        sums_kernel,
        (
            pltpu.VMEM((2 * STATE + 8, FEATS), f32),
            wide, wide, wide, wide, wide, thin, thin,
            pltpu.VMEM((HEADS_DEV, length), f32),
        ),
        [IN_HBM, IN_HBM, IN_HBM, IN_HBM, IN_VMEM, IN_SMEM],
        [pltpu.VMEM((length, FEATS), bf16), pltpu.SemaphoreType.DMA((CHUNKS, 4))],
        flops=1 << 30,
    )(inputs, upstream, write_proj, read_proj, step_size.T, decay_rate)

    swap = [(i, i ^ 1) for i in range(2 * CHIPS)]

    def fan(hop):
        up = [(2 * z, 2 * ((z + hop) % CHIPS)) for z in range(CHIPS)]
        down = [(2 * z + 1, 2 * ((z - hop) % CHIPS) + 1) for z in range(CHIPS)]
        return up + down

    other = lax.ppermute(own, "ctx", swap)
    message = jax.ShapeDtypeStruct((STATE + 8, FEATS), f32)
    messages = call(
        message_kernel,
        (message, message, message, jax.ShapeDtypeStruct((STATE + 8, FEATS // 2), f32)),
        [IN_VMEM, IN_VMEM],
        [pltpu.VMEM((STATE, FEATS), f32), pltpu.VMEM((STATE, FEATS), f32)],
        flops=1 << 20,
    )(own, other)
    mine = [lax.ppermute(m, "ctx", fan(hop)) for m, hop in zip(messages, (1, 2, 3, FAR))]
    theirs = [lax.ppermute(m, "ctx", swap) for m in mine]

    gi, back, pw, pr, init_t = call(
        local_kernel,
        (wide32, wide32, thin32, thin32, pltpu.VMEM((STATE, FEATS), f32)),
        [IN_VMEM] * 8 + [IN_SMEM, IN_VMEM],
        flops=5 << 30,
    )(xdh, xdl, xuh, xul, dy, w, r, bt, skip_gain, init_state)

    rows = call(
        finish_kernel,
        jax.ShapeDtypeStruct((length, FEATS + 2 * STATE), bf16),
        [IN_VMEM] * 20,
        [pltpu.VMEM((2 * STATE, FEATS), bf16), pltpu.VMEM((2 * STATE, FEATS), bf16)],
        flops=1 << 30,
    )(own, other, *mine, *theirs, xdh, xdl, xuh, xul, w, gi, back, pw, pr, init_t)

    moved = lax.all_to_all(rows, "head", split_axis=0, concat_axis=0, tiled=True)
    share = length // lax.axis_size("head")
    return call(
        arrange_kernel,
        (
            jax.ShapeDtypeStruct((share, HEADS * HEAD_SIZE), bf16),
            jax.ShapeDtypeStruct((share, GROUPS * STATE), bf16),
            jax.ShapeDtypeStruct((share, GROUPS * STATE), bf16),
        ),
        [IN_VMEM],
    )(moved)


def solution(mesh):
    placed = (
        P("ctx", "head"),
        P("ctx", "head"),
        P("ctx", "head"),
        P("head"),
        P("ctx", None),
        P("ctx", None),
        P("head", None, None),
        P("head"),
    )
    return jax.shard_map(
        per_device,
        mesh=mesh,
        in_specs=placed,
        out_specs=(P(("ctx", "head"), None), P(("ctx", "head"), None), P(("ctx", "head"), None)),
        check_vma=False,
    )
```

```python
import functools

import jax
import jax.numpy as jnp
from jax import lax
from jax.experimental import pallas as pl
from jax.experimental.pallas import tpu as pltpu
from jax.sharding import PartitionSpec as P

HEADS = 128
HEAD_SIZE = 64
STATE = 128
GROUPS = 8
TOKENS_DEV = 1024
HEADS_DEV = 8
FEATS = HEADS_DEV * HEAD_SIZE
CHUNK = 256
CHUNKS = TOKENS_DEV // CHUNK
CHIPS = 8
FAR = CHIPS // 2
ROWS = STATE + 16
LEAST = 1e-30
CUT = 2

f32 = jnp.float32
bf16 = jnp.bfloat16
VMEM_LIMIT = 40 * 1024 * 1024


def nn(a, b):
    return lax.dot_general(a, b, (((1,), (0,)), ((), ())), preferred_element_type=f32)


def nt(a, b):
    return lax.dot_general(a, b, (((1,), (1,)), ((), ())), preferred_element_type=f32)


def tn(a, b):
    return lax.dot_general(a, b, (((0,), (0,)), ((), ())), preferred_element_type=f32)


def halves(x):
    high = x.astype(bf16)
    return high, (x - high.astype(f32)).astype(bf16)


def head_columns():
    row = lax.broadcasted_iota(jnp.int32, (3 * HEADS_DEV, FEATS), 0) % HEADS_DEV
    col = lax.broadcasted_iota(jnp.int32, (3 * HEADS_DEV, FEATS), 1) // HEAD_SIZE
    return jnp.where(row == col, 1.0, 0.0).astype(bf16)


def spread(per_head, columns):
    high = per_head.astype(bf16).astype(f32)
    rest = per_head - high
    mid = rest.astype(bf16).astype(f32)
    low = rest - mid
    return tn(jnp.concatenate([high, mid, low], axis=0).astype(bf16), columns)


def head_vector(ref):
    row = lax.broadcasted_iota(jnp.int32, (HEADS_DEV, STATE), 0)
    out = jnp.zeros((HEADS_DEV, STATE), f32)
    for h in range(HEADS_DEV):
        out = jnp.where(row == h, ref[h], out)
    return out


def cumulate(x):
    lane = lax.broadcasted_iota(jnp.int32, x.shape, 1)
    hop = 1
    while hop < x.shape[1]:
        x = x + jnp.where(lane >= hop, pltpu.roll(x, hop, 1), 0.0)
        hop *= 2
    return x


def rows_of(i):
    return pl.ds(i * CHUNK, CHUNK)


def sums_kernel(
    u_hbm, dy_hbm, w_hbm, r_hbm, step_hbm, rate_hbm,
    out_ref, xdh_ref, xdl_ref, xuh_ref, xul_ref, dy_ref, w_ref, r_ref, bt_ref,
    u_ref, step_ref, rate_ref, sems,
):
    column = pl.multiple_of(lax.axis_index("head") // 2 * STATE, STATE)
    small = [
        pltpu.make_async_copy(step_hbm, step_ref, sems.at[CHUNKS, 0]),
        pltpu.make_async_copy(rate_hbm, rate_ref, sems.at[CHUNKS, 1]),
    ]
    for copy in small:
        copy.start()
    copies = []
    for i in range(CHUNKS):
        rows = rows_of(i)
        group = [
            pltpu.make_async_copy(u_hbm.at[rows, :], u_ref.at[rows, :], sems.at[i, 0]),
            pltpu.make_async_copy(dy_hbm.at[rows, :], dy_ref.at[rows, :], sems.at[i, 1]),
            pltpu.make_async_copy(w_hbm.at[rows, pl.ds(column, STATE)], w_ref.at[rows, :], sems.at[i, 2]),
            pltpu.make_async_copy(r_hbm.at[rows, pl.ds(column, STATE)], r_ref.at[rows, :], sems.at[i, 3]),
        ]
        for copy in group:
            copy.start()
        copies.append(group)
    columns = head_columns()
    for copy in small:
        copy.wait()
    steps = step_ref[...]
    rate = head_vector(rate_ref)[:, :1]
    cum = cumulate(-steps * rate)
    last = cum[:, TOKENS_DEV - 1 :]
    middle = 0.5 * last
    ahead = jnp.exp(cum - middle)
    behind = jnp.exp(middle - cum) * steps
    bt_ref[...] = behind
    wide = lambda x: spread(jnp.broadcast_to(x, (HEADS_DEV, STATE)), columns)
    half = wide(jnp.exp(middle))
    acc_w = jnp.zeros((STATE, FEATS), f32)
    acc_r = jnp.zeros((STATE, FEATS), f32)
    for i in range(CHUNKS):
        rows = rows_of(i)
        for copy in copies[i]:
            copy.wait()
        high, low = halves(spread(behind[:, i * CHUNK : (i + 1) * CHUNK], columns) * u_ref[rows, :].astype(f32))
        xuh_ref[rows, :] = high
        xul_ref[rows, :] = low
        writes = w_ref[rows, :]
        acc_w = acc_w + tn(writes, high) + tn(writes, low)
        high, low = halves(spread(ahead[:, i * CHUNK : (i + 1) * CHUNK], columns) * dy_ref[rows, :].astype(f32))
        xdh_ref[rows, :] = high
        xdl_ref[rows, :] = low
        reads = r_ref[rows, :]
        acc_r = acc_r + tn(reads, high) + tn(reads, low)
    out_ref[pl.ds(0, STATE), :] = half * acc_w
    out_ref[pl.ds(STATE, STATE), :] = half * acc_r
    out_ref[pl.ds(2 * STATE, 8), :] = wide(last)[:8, :]


def parts_of(x):
    high = x.astype(bf16).astype(f32)
    mid = (x - high).astype(bf16).astype(f32)
    return [high, mid, x - high - mid]


def message_kernel(own_ref, other_ref, a_ref, b_ref, c_ref, far_ref, w_ref, r_ref):
    place = lax.axis_index("ctx")
    chip, core = place // 2, place % 2
    own_log = own_ref[pl.ds(2 * STATE, 1), :]
    other_log = other_ref[pl.ds(2 * STATE, 1), :]
    own_decay = jnp.exp(own_log)
    other_decay = jnp.exp(other_log)
    first = core == 0
    one = jnp.ones_like(own_decay)
    logs = parts_of(own_log + other_log)
    for ref, left, right, at in (
        (w_ref, jnp.where(first, other_decay, one), jnp.where(first, one, own_decay), 0),
        (r_ref, jnp.where(first, one, other_decay), jnp.where(first, own_decay, one), STATE),
    ):
        rows = pl.ds(at, STATE)
        total = left * own_ref[rows, :] + right * other_ref[rows, :]
        scale = jnp.maximum(jnp.max(jnp.abs(total), axis=0, keepdims=True), LEAST)
        ref[pl.ds(0, STATE), :] = total * (1.0 / scale)
        ref[pl.ds(STATE, 16), :] = jnp.concatenate(
            logs + parts_of(jnp.log(scale)) + [jnp.zeros((10, FEATS), f32)], axis=0
        )
    for hop, ref in ((1, a_ref), (2, b_ref), (3, c_ref)):
        to_later = jnp.where(first, chip + hop < CHIPS, chip - hop < 0)

        @pl.when(to_later)
        def _():
            ref[...] = w_ref[...]

        @pl.when(jnp.logical_not(to_later))
        def _():
            ref[...] = r_ref[...]

    half = FEATS // 2
    later = chip < FAR
    for part in range(2):
        cols = pl.ds(part * half, half)

        @pl.when(jnp.logical_and(later, core == part))
        def _():
            far_ref[...] = w_ref[:, cols]

        @pl.when(jnp.logical_and(jnp.logical_not(later), core == part))
        def _():
            far_ref[...] = r_ref[:, cols]


def local_kernel(parts, *refs):
    first = 0 in parts
    xdh_ref, xdl_ref, xuh_ref, xul_ref, dy_ref, w_ref, r_ref, bt_ref, skip_ref = refs[:9]
    gi_ref, back_ref, pw_ref, pr_ref = refs[10:14]
    columns = head_columns()
    skip = spread(head_vector(skip_ref), columns)[:1, :]
    if first:
        refs[14][...] = refs[9][...].reshape(FEATS, STATE).T
    row = lax.broadcasted_iota(jnp.int32, (CHUNK, CHUNK), 0)
    col = lax.broadcasted_iota(jnp.int32, (CHUNK, CHUNK), 1)
    keep = col >= row
    base = parts[0]
    for j in parts:
        to, out = rows_of(j), rows_of(j - base)
        writes = w_ref[to, :]
        uh, ul = xuh_ref[to, :], xul_ref[to, :]
        acc_gi = jnp.zeros((CHUNK, FEATS), f32)
        acc_pw = jnp.zeros((CHUNK, STATE), f32)
        for i in range(j, CHUNKS):
            at, into = rows_of(i), rows_of(i - base)
            dh, dl = xdh_ref[at, :], xdl_ref[at, :]
            reads = r_ref[at, :]
            pairs = nt(uh, dh) + nt(uh, dl) + nt(ul, dh)
            dots = nt(writes, reads)
            if i == j:
                pairs = jnp.where(keep, pairs, 0.0)
                dots = jnp.where(keep, dots, 0.0)
            ph, plow = halves(pairs)
            gh, gl = halves(dots)
            acc_pw = acc_pw + nn(ph, reads) + nn(plow, reads)
            part = tn(ph, writes) + tn(plow, writes)
            pr_ref[into, :] = part if j == base else pr_ref[into, :] + part
            acc_gi = acc_gi + nn(gh, dh) + nn(gh, dl) + nn(gl, dh)
        back = spread(bt_ref[:, j * CHUNK : (j + 1) * CHUNK], columns)
        back_ref[out, :] = back
        gi_ref[out, :] = back * acc_gi + skip * dy_ref[to, :].astype(f32)
        pw_ref[out, :] = acc_pw


def finish_kernel(
    own_ref, other_ref, a_ref, b_ref, c_ref, far_ref, oa_ref, ob_ref, oc_ref, ofar_ref,
    xdh_ref, xdl_ref, xuh_ref, xul_ref, w_ref, gi1_ref, back1_ref, pw1_ref, pr1_ref, init_t_ref,
    gi2_ref, back2_ref, pw2_ref, pr2_ref, rows_ref, s_ref, t_ref,
):
    place = lax.axis_index("ctx")
    chip, core = place // 2, place % 2
    first = core == 0

    def pick(rows, hop):
        mine = (a_ref, b_ref, c_ref)[hop - 1][rows, :]
        theirs = (oa_ref, ob_ref, oc_ref)[hop - 1][rows, :]
        return jnp.where(first, mine, theirs), jnp.where(first, theirs, mine)

    def pick_far(rows):
        mine, theirs = far_ref[rows, :], ofar_ref[rows, :]
        return jnp.concatenate(
            [jnp.where(first, mine, theirs), jnp.where(first, theirs, mine)], axis=1
        )

    def distant(rows):
        below, above = {}, {}
        for hop in range(1, FAR):
            low, high = pick(rows, hop)
            below[hop], above[CHIPS - hop] = low, low
            above[hop], below[CHIPS - hop] = high, high
        middle = pick_far(rows)
        below[FAR], above[FAR] = middle, middle
        return below, above

    below, above = distant(pl.ds(STATE, 8))
    weights_s, weights_a = {}, {}

    def logs(rows):
        return rows[0:1] + rows[1:2] + rows[2:3], rows[3:4] + rows[4:5] + rows[5:6]

    total = jnp.zeros((1, FEATS), f32)
    for hop in range(1, CHIPS):
        valid = chip - hop >= 0
        decay, scale = logs(below[hop])
        weights_s[hop] = jnp.where(valid, jnp.exp(total + scale), 0.0)
        total = total + jnp.where(valid, decay, 0.0)
    weight_init = jnp.exp(total)
    total = jnp.zeros((1, FEATS), f32)
    for hop in range(1, CHIPS):
        valid = chip + hop < CHIPS
        decay, scale = logs(above[hop])
        weights_a[hop] = jnp.where(valid, jnp.exp(total + scale), 0.0)
        total = total + jnp.where(valid, decay, 0.0)

    own_log = own_ref[pl.ds(2 * STATE, 1), :]
    other_decay = jnp.exp(other_ref[pl.ds(2 * STATE, 1), :])
    half = jnp.exp(0.5 * own_log)
    for at in range(0, STATE, 32):
        rows = pl.ds(at, 32)
        below, above = distant(rows)
        state = weight_init * init_t_ref[rows, :]
        adjoint = jnp.zeros((32, FEATS), f32)
        for hop in range(1, CHIPS):
            state = state + weights_s[hop] * below[hop]
            adjoint = adjoint + weights_a[hop] * above[hop]
        state = jnp.where(first, state, other_ref[rows, :] + other_decay * state)
        adjoint = jnp.where(
            first, other_ref[pl.ds(STATE + at, 32), :] + other_decay * adjoint, adjoint
        )
        high, low = halves(half * state)
        s_ref[rows, :] = high
        s_ref[pl.ds(STATE + at, 32), :] = low
        high, low = halves(half * adjoint)
        t_ref[rows, :] = high
        t_ref[pl.ds(STATE + at, 32), :] = low

    for i in range(CHUNKS):
        rows = rows_of(i)
        reads = nt(xdh_ref[rows, :], s_ref[...])
        reads = reads[:, :STATE] + reads[:, STATE:] + nt(xdl_ref[rows, :], s_ref[pl.ds(0, STATE), :])
        writes = nt(xuh_ref[rows, :], t_ref[...])
        writes = writes[:, :STATE] + writes[:, STATE:] + nt(xul_ref[rows, :], t_ref[pl.ds(0, STATE), :])
        vectors = w_ref[rows, :]
        through = nn(jnp.concatenate([vectors, vectors], axis=1), t_ref[...])
        early = i < CUT
        gi_ref, back_ref, pw_ref = (gi1_ref, back1_ref, pw1_ref) if early else (gi2_ref, back2_ref, pw2_ref)
        at = rows_of(i if early else i - CUT)
        reads = reads + pr1_ref[rows, :]
        if not early:
            reads = reads + pr2_ref[at, :]
        rows_ref[rows, pl.ds(0, FEATS)] = (gi_ref[at, :] + back_ref[at, :] * through).astype(bf16)
        rows_ref[rows, pl.ds(FEATS, STATE)] = (pw_ref[at, :] + writes).astype(bf16)
        rows_ref[rows, pl.ds(FEATS + STATE, STATE)] = reads.astype(bf16)


def relay_kernel(*refs):
    pass


def arrange_kernel(in_ref, gi_ref, gw_ref, gr_ref):
    share = gi_ref.shape[0]
    peers = in_ref.shape[0] // share
    for j in range(peers):
        gi_ref[:, pl.ds(j * FEATS, FEATS)] = in_ref[pl.ds(j * share, share), pl.ds(0, FEATS)]
    for g in range(GROUPS):
        one, two = pl.ds(2 * g * share, share), pl.ds((2 * g + 1) * share, share)
        for ref, at in ((gw_ref, FEATS), (gr_ref, FEATS + STATE)):
            cols = pl.ds(at, STATE)
            ref[:, pl.ds(g * STATE, STATE)] = (
                in_ref[one, cols].astype(f32) + in_ref[two, cols].astype(f32)
            ).astype(bf16)


def call(body, outs, ins, scratch=(), flops=0):
    return pl.pallas_call(
        body,
        out_shape=outs,
        in_specs=ins,
        scratch_shapes=scratch,
        compiler_params=pltpu.CompilerParams(vmem_limit_bytes=VMEM_LIMIT),
        cost_estimate=pl.CostEstimate(flops=flops, bytes_accessed=1 << 20, transcendentals=0),
    )


IN_HBM = pl.BlockSpec(memory_space=pltpu.HBM)
IN_ANY = pl.BlockSpec(memory_space=pl.ANY)
IN_VMEM = pl.BlockSpec(memory_space=pltpu.VMEM)
IN_SMEM = pl.BlockSpec(memory_space=pltpu.SMEM)


def per_device(inputs, upstream, step_size, decay_rate, write_proj, read_proj, init_state, skip_gain):
    length = TOKENS_DEV
    wide = pltpu.VMEM((length, FEATS), bf16)
    wide32 = pltpu.VMEM((length, FEATS), f32)
    thin = pltpu.VMEM((length, STATE), bf16)
    thin32 = pltpu.VMEM((length, STATE), f32)
    own, xdh, xdl, xuh, xul, dy, w, r, bt = call(
        sums_kernel,
        (
            pltpu.VMEM((2 * STATE + 8, FEATS), f32),
            wide, wide, wide, wide, wide, thin, thin,
            pltpu.VMEM((HEADS_DEV, length), f32),
        ),
        [IN_HBM] * 6,
        [
            pltpu.VMEM((length, FEATS), bf16),
            pltpu.VMEM((HEADS_DEV, length), f32),
            pltpu.SMEM((HEADS_DEV,), f32),
            pltpu.SemaphoreType.DMA((CHUNKS + 1, 4)),
        ],
        flops=1 << 30,
    )(
        *(
            pltpu.with_memory_space_constraint(a, pltpu.HBM)
            for a in (inputs, upstream, write_proj, read_proj, step_size.T, decay_rate)
        )
    )

    swap = [(i, i ^ 1) for i in range(2 * CHIPS)]

    def fan(hop):
        up = [(2 * z, 2 * ((z + hop) % CHIPS)) for z in range(CHIPS)]
        down = [(2 * z + 1, 2 * ((z - hop) % CHIPS) + 1) for z in range(CHIPS)]
        return up + down

    other = lax.ppermute(own, "ctx", swap)
    message = jax.ShapeDtypeStruct((ROWS, FEATS), f32)
    messages = call(
        message_kernel,
        (message, message, message, jax.ShapeDtypeStruct((ROWS, FEATS // 2), f32)),
        [IN_VMEM, IN_VMEM],
        [pltpu.VMEM((ROWS, FEATS), f32), pltpu.VMEM((ROWS, FEATS), f32)],
        flops=1 << 20,
    )(own, other)
    mine = [
        lax.ppermute(m.astype(jnp.float16), "ctx", fan(hop)).astype(f32)
        for m, hop in zip(messages, (1, 2, 3, FAR))
    ]

    def local(parts, flops):
        out = lambda n, d: pltpu.VMEM((CHUNK * n, d), f32)
        n = len(parts)
        left = CHUNKS - parts[0]
        outs = (out(n, FEATS), out(n, FEATS), out(n, STATE), out(left, STATE))
        if 0 in parts:
            outs = outs + (pltpu.VMEM((STATE, FEATS), f32),)
        return call(
            functools.partial(local_kernel, parts), outs, [IN_VMEM] * 8 + [IN_SMEM, IN_VMEM], flops=flops
        )(xdh, xdl, xuh, xul, dy, w, r, bt, skip_gain, init_state)

    early = local(tuple(range(CUT)), 4 << 30)
    late = local(tuple(range(CUT, CHUNKS)), 2 << 30)
    relayed = pl.pallas_call(
        relay_kernel,
        out_shape=tuple(jax.ShapeDtypeStruct(m.shape, m.dtype) for m in mine),
        in_specs=[IN_ANY] * 5,
        out_specs=(IN_ANY,) * 4,
        input_output_aliases={i: i for i in range(4)},
    )(*mine, early[2])
    mine = list(relayed)
    theirs = [lax.ppermute(m, "ctx", swap) for m in mine]

    rows = call(
        finish_kernel,
        jax.ShapeDtypeStruct((length, FEATS + 2 * STATE), bf16),
        [IN_VMEM] * 24,
        [pltpu.VMEM((2 * STATE, FEATS), bf16), pltpu.VMEM((2 * STATE, FEATS), bf16)],
        flops=1 << 30,
    )(own, other, *mine, *theirs, xdh, xdl, xuh, xul, w, *early, *late)

    moved = lax.all_to_all(rows, "head", split_axis=0, concat_axis=0, tiled=True)
    share = length // lax.axis_size("head")
    return call(
        arrange_kernel,
        (
            jax.ShapeDtypeStruct((share, HEADS * HEAD_SIZE), bf16),
            jax.ShapeDtypeStruct((share, GROUPS * STATE), bf16),
            jax.ShapeDtypeStruct((share, GROUPS * STATE), bf16),
        ),
        [IN_VMEM],
    )(moved)


def solution(mesh):
    placed = (
        P("ctx", "head"),
        P("ctx", "head"),
        P("ctx", "head"),
        P("head"),
        P("ctx", None),
        P("ctx", None),
        P("head", None, None),
        P("head"),
    )
    return jax.shard_map(
        per_device,
        mesh=mesh,
        in_specs=placed,
        out_specs=(P(("ctx", "head"), None), P(("ctx", "head"), None), P(("ctx", "head"), None)),
        check_vma=False,
    )
```

```python
import functools

import jax
import jax.numpy as jnp
from jax import lax
from jax.experimental import pallas as pl
from jax.experimental.pallas import tpu as pltpu
from jax.sharding import PartitionSpec as P

HEADS = 128
HEAD_SIZE = 64
STATE = 128
GROUPS = 8
TOKENS_DEV = 1024
HEADS_DEV = 8
FEATS = HEADS_DEV * HEAD_SIZE
CHUNK = 256
CHUNKS = TOKENS_DEV // CHUNK
CHIPS = 8
FAR = CHIPS // 2
ROWS = STATE + 8
LEAST = 1e-30

f32 = jnp.float32
bf16 = jnp.bfloat16
VMEM_LIMIT = 12 * 1024 * 1024


def nn(a, b):
    return lax.dot_general(a, b, (((1,), (0,)), ((), ())), preferred_element_type=f32)


def nt(a, b):
    return lax.dot_general(a, b, (((1,), (1,)), ((), ())), preferred_element_type=f32)


def tn(a, b):
    return lax.dot_general(a, b, (((0,), (0,)), ((), ())), preferred_element_type=f32)


def halves(x):
    high = x.astype(bf16)
    return high, (x - high.astype(f32)).astype(bf16)


def parts_of(x):
    high = x.astype(bf16).astype(f32)
    mid = (x - high).astype(bf16).astype(f32)
    return [high, mid, x - high - mid]


def head_columns():
    row = lax.broadcasted_iota(jnp.int32, (3 * HEADS_DEV, FEATS), 0) % HEADS_DEV
    col = lax.broadcasted_iota(jnp.int32, (3 * HEADS_DEV, FEATS), 1) // HEAD_SIZE
    return jnp.where(row == col, 1.0, 0.0).astype(bf16)


def spread(per_head, columns):
    high = per_head.astype(bf16).astype(f32)
    rest = per_head - high
    mid = rest.astype(bf16).astype(f32)
    low = rest - mid
    return tn(jnp.concatenate([high, mid, low], axis=0).astype(bf16), columns)


def head_vector(ref):
    row = lax.broadcasted_iota(jnp.int32, (HEADS_DEV, STATE), 0)
    out = jnp.zeros((HEADS_DEV, STATE), f32)
    for h in range(HEADS_DEV):
        out = jnp.where(row == h, ref[h], out)
    return out


def cumulate(x):
    width = 128
    runs = x.shape[1] // width
    stacked = jnp.concatenate([x[:, k * width : (k + 1) * width] for k in range(runs)], axis=0)
    row = lax.broadcasted_iota(jnp.int32, (width, width), 0)
    col = lax.broadcasted_iota(jnp.int32, (width, width), 1)
    ones = jnp.where(row <= col, 1.0, 0.0).astype(bf16)
    parts = jnp.concatenate(parts_of(stacked), axis=1).astype(bf16)
    inner = nn(parts, jnp.concatenate([ones] * 3, axis=0))
    out, offset = [], jnp.zeros((HEADS_DEV, width), f32)
    for k in range(runs):
        run = inner[k * HEADS_DEV : (k + 1) * HEADS_DEV]
        out.append(run + offset)
        offset = offset + jnp.broadcast_to(run[:, width - 1 :], (HEADS_DEV, width))
    return jnp.concatenate(out, axis=1)


def rows_of(i):
    return pl.ds(i * CHUNK if isinstance(i, int) else pl.multiple_of(i * CHUNK, CHUNK), CHUNK)


def slot(i):
    return pl.ds(i * STATE if isinstance(i, int) else pl.multiple_of(i * STATE, STATE), STATE)


def sums_kernel(
    u_hbm, dy_hbm, w_hbm, r_hbm, step_hbm, rate_hbm,
    out_ref, xdh_ref, xdl_ref, xuh_ref, xul_ref, dy_ref, w_ref, r_ref, bt_ref, early_ref, late_ref,
    u_ref, at_ref, step_ref, rate_ref, sems,
):
    column = pl.multiple_of(lax.axis_index("head") // 2 * STATE, STATE)
    small = [
        pltpu.make_async_copy(step_hbm, step_ref, sems.at[CHUNKS, 0]),
        pltpu.make_async_copy(rate_hbm, rate_ref, sems.at[CHUNKS, 1]),
    ]
    for copy in small:
        copy.start()

    def copies(k):
        rows, back = rows_of(k), rows_of(CHUNKS - 1 - k)
        return [
            pltpu.make_async_copy(u_hbm.at[rows, :], u_ref.at[rows, :], sems.at[k, 0]),
            pltpu.make_async_copy(w_hbm.at[rows, pl.ds(column, STATE)], w_ref.at[rows, :], sems.at[k, 1]),
            pltpu.make_async_copy(dy_hbm.at[back, :], dy_ref.at[back, :], sems.at[k, 2]),
            pltpu.make_async_copy(r_hbm.at[back, pl.ds(column, STATE)], r_ref.at[back, :], sems.at[k, 3]),
        ]

    for k in range(CHUNKS):
        for copy in copies(k):
            copy.start()
    columns = head_columns()
    for copy in small:
        copy.wait()
    steps = step_ref[...]
    rate = head_vector(rate_ref)[:, :1]
    cum = cumulate(-steps * rate)
    last = cum[:, TOKENS_DEV - 1 :]
    middle = 0.5 * last
    ahead = jnp.exp(cum - middle)
    at_ref[...] = ahead
    bt_ref[...] = jnp.exp(middle - cum) * steps
    wide = lambda x: spread(jnp.broadcast_to(x, (HEADS_DEV, STATE)), columns)
    half = wide(jnp.exp(middle))
    early_ref[pl.ds(0, STATE), :] = jnp.zeros((STATE, FEATS), f32)
    late_ref[pl.ds(CHUNKS * STATE, STATE), :] = jnp.zeros((STATE, FEATS), f32)

    def weigh(per_head_ref, i, values, high_ref, low_ref, vectors):
        rows = rows_of(i)
        weights = spread(per_head_ref[:, rows], columns)
        high, low = halves(weights * values[rows, :].astype(f32))
        high_ref[rows, :] = high
        low_ref[rows, :] = low
        both = tn(vectors[rows, :], jnp.concatenate([high, low], axis=1))
        return both[:, :FEATS] + both[:, FEATS:]

    def step(k):
        for copy in copies(k):
            copy.wait()
        early_ref[slot(k + 1), :] = early_ref[slot(k), :] + weigh(bt_ref, k, u_ref, xuh_ref, xul_ref, w_ref)
        i = CHUNKS - 1 - k
        late_ref[slot(i), :] = late_ref[slot(i + 1), :] + weigh(at_ref, i, dy_ref, xdh_ref, xdl_ref, r_ref)

    for k in range(CHUNKS):
        step(k)
    out_ref[pl.ds(0, STATE), :] = half * early_ref[slot(CHUNKS), :]
    out_ref[pl.ds(STATE, STATE), :] = half * late_ref[slot(0), :]
    out_ref[pl.ds(2 * STATE, 8), :] = wide(last)[:8, :]


def message_kernel(own_ref, other_ref, a_ref, b_ref, c_ref, far_ref, w_ref, r_ref):
    place = lax.axis_index("ctx")
    chip, core = place // 2, place % 2
    own_log = own_ref[pl.ds(2 * STATE, 1), :]
    other_log = other_ref[pl.ds(2 * STATE, 1), :]
    own_decay = jnp.exp(own_log)
    other_decay = jnp.exp(other_log)
    first = core == 0
    one = jnp.ones_like(own_decay)
    logs = parts_of(own_log + other_log)
    for ref, left, right, at in (
        (w_ref, jnp.where(first, other_decay, one), jnp.where(first, one, own_decay), 0),
        (r_ref, jnp.where(first, one, other_decay), jnp.where(first, own_decay, one), STATE),
    ):
        rows = pl.ds(at, STATE)
        total = left * own_ref[rows, :] + right * other_ref[rows, :]
        scale = jnp.maximum(jnp.max(jnp.abs(total), axis=0, keepdims=True), LEAST)
        ref[pl.ds(0, STATE), :] = total * (1.0 / scale)
        ref[pl.ds(STATE, 8), :] = jnp.concatenate(
            logs + parts_of(jnp.log(scale)) + [jnp.zeros((2, FEATS), f32)], axis=0
        )
    for hop, ref in ((1, a_ref), (2, b_ref), (3, c_ref)):
        to_later = jnp.where(first, chip + hop < CHIPS, chip - hop < 0)

        @pl.when(to_later)
        def _():
            ref[...] = w_ref[...]

        @pl.when(jnp.logical_not(to_later))
        def _():
            ref[...] = r_ref[...]

    half = FEATS // 2
    later = chip < FAR
    for part in range(2):
        cols = pl.ds(part * half, half)

        @pl.when(jnp.logical_and(later, core == part))
        def _():
            far_ref[...] = w_ref[:, cols]

        @pl.when(jnp.logical_and(jnp.logical_not(later), core == part))
        def _():
            far_ref[...] = r_ref[:, cols]


def local_kernel(
    xdh_ref, xdl_ref, xuh_ref, xul_ref, dy_ref, w_ref, r_ref, bt_ref, skip_ref, init_ref,
    gi_ref, back_ref, pw_ref, pr_ref, init_t_ref,
):
    columns = head_columns()
    skip = spread(head_vector(skip_ref), columns)[:1, :]
    init_t_ref[...] = init_ref[...].reshape(FEATS, STATE).T
    row = lax.broadcasted_iota(jnp.int32, (CHUNK, CHUNK), 0)
    col = lax.broadcasted_iota(jnp.int32, (CHUNK, CHUNK), 1)
    keep = col >= row
    for i in range(CHUNKS):
        rows = rows_of(i)
        writes, reads = w_ref[rows, :], r_ref[rows, :]
        uh, ul = xuh_ref[rows, :], xul_ref[rows, :]
        dh, dl = xdh_ref[rows, :], xdl_ref[rows, :]
        pairs = nt(jnp.concatenate([uh, uh, ul], axis=1), jnp.concatenate([dh, dl, dh], axis=1))
        ph, plow = halves(jnp.where(keep, pairs, 0.0))
        gh, gl = halves(jnp.where(keep, nt(writes, reads), 0.0))
        total = nn(jnp.concatenate([gh, gh, gl], axis=1), jnp.concatenate([dh, dl, dh], axis=0))
        back = spread(bt_ref[:, i * CHUNK : (i + 1) * CHUNK], columns)
        back_ref[rows, :] = back
        gi_ref[rows, :] = back * total + skip * dy_ref[rows, :].astype(f32)
        pw_ref[rows, :] = nn(ph, reads) + nn(plow, reads)
        pr_ref[rows, :] = tn(ph, writes) + tn(plow, writes)


def finish_kernel(
    own_ref, other_ref, a_ref, b_ref, c_ref, far_ref, oa_ref, ob_ref, oc_ref, ofar_ref,
    xdh_ref, xdl_ref, xuh_ref, xul_ref, w_ref, early_ref, late_ref,
    gi_ref, back_ref, pw_ref, pr_ref, init_t_ref,
    rows_ref, s_ref, t_ref, states_ref, adjoints_ref,
):
    place = lax.axis_index("ctx")
    chip, core = place // 2, place % 2
    first = core == 0
    mine, theirs = (a_ref, b_ref, c_ref), (oa_ref, ob_ref, oc_ref)

    logs_at = pl.ds(STATE, 8)

    def logs(rows):
        return rows[0:1] + rows[1:2] + rows[2:3], rows[3:4] + rows[4:5] + rows[5:6]

    below, above = {}, {}
    for hop in range(1, FAR):
        own_rows, other_rows = mine[hop - 1][logs_at, :], theirs[hop - 1][logs_at, :]
        low, high = jnp.where(first, own_rows, other_rows), jnp.where(first, other_rows, own_rows)
        below[hop] = above[CHIPS - hop] = logs(low)
        above[hop] = below[CHIPS - hop] = logs(high)
    own_rows, other_rows = far_ref[logs_at, :], ofar_ref[logs_at, :]
    below[FAR] = above[FAR] = logs(
        jnp.concatenate(
            [jnp.where(first, own_rows, other_rows), jnp.where(first, other_rows, own_rows)], axis=1
        )
    )

    def weigh(table, inside):
        weights, total = {}, jnp.zeros((1, FEATS), f32)
        for hop in range(1, CHIPS):
            decay, scale = table[hop]
            weights[hop] = jnp.where(inside(hop), jnp.exp(total + scale), 0.0)
            total = total + jnp.where(inside(hop), decay, 0.0)
        return weights, total

    to_state, total = weigh(below, lambda hop: chip - hop >= 0)
    to_adjoint, _ = weigh(above, lambda hop: chip + hop < CHIPS)
    weight_init = jnp.exp(total)
    terms = []
    for hop in range(1, FAR):
        low = to_state[hop], to_adjoint[CHIPS - hop]
        high = to_state[CHIPS - hop], to_adjoint[hop]
        for ref, own in ((mine[hop - 1], True), (theirs[hop - 1], False)):
            one, two = (low, high) if own else (high, low)
            terms.append((ref, jnp.where(first, one[0], two[0]), jnp.where(first, one[1], two[1])))

    own_log = own_ref[pl.ds(2 * STATE, 1), :]
    other_decay = jnp.exp(other_ref[pl.ds(2 * STATE, 1), :])
    half = jnp.exp(0.5 * own_log)
    keep_s = jnp.where(first, half, half * other_decay)
    keep_a = jnp.where(first, half * other_decay, half)
    add_s = jnp.where(first, 0.0, half)
    add_a = jnp.where(first, half, 0.0)
    step = 32
    for at in range(0, STATE, step):
        rows = pl.ds(at, step)
        near, distant = far_ref[rows, :], ofar_ref[rows, :]
        middle = jnp.concatenate(
            [jnp.where(first, near, distant), jnp.where(first, distant, near)], axis=1
        )
        state = weight_init * init_t_ref[rows, :] + to_state[FAR] * middle
        adjoint = to_adjoint[FAR] * middle
        for ref, for_state, for_adjoint in terms:
            value = ref[rows, :]
            state = state + for_state * value
            adjoint = adjoint + for_adjoint * value
        states_ref[rows, :] = keep_s * state + add_s * other_ref[rows, :]
        adjoints_ref[rows, :] = keep_a * adjoint + add_a * other_ref[pl.ds(STATE + at, step), :]

    for i in range(CHUNKS):
        rows = rows_of(i)
        base = i * 2 * STATE
        state = states_ref[...] + early_ref[slot(i), :]
        adjoint = adjoints_ref[...] + late_ref[slot(i + 1), :]
        sh, sl = halves(state)
        th, tl = halves(adjoint)
        s_ref[pl.ds(base, STATE), :] = sh
        s_ref[pl.ds(base + STATE, STATE), :] = sl
        t_ref[pl.ds(base, STATE), :] = th
        t_ref[pl.ds(base + STATE, STATE), :] = tl
        both, high = pl.ds(base, 2 * STATE), pl.ds(base, STATE)
        reads = nt(xdh_ref[rows, :], s_ref[both, :])
        reads = reads[:, :STATE] + reads[:, STATE:] + nt(xdl_ref[rows, :], s_ref[high, :])
        writes = nt(xuh_ref[rows, :], t_ref[both, :])
        writes = writes[:, :STATE] + writes[:, STATE:] + nt(xul_ref[rows, :], t_ref[high, :])
        vectors = w_ref[rows, :]
        through = nn(jnp.concatenate([vectors, vectors], axis=1), t_ref[both, :])
        rows_ref[rows, pl.ds(0, FEATS)] = (gi_ref[rows, :] + back_ref[rows, :] * through).astype(bf16)
        rows_ref[rows, pl.ds(FEATS, STATE)] = (pw_ref[rows, :] + writes).astype(bf16)
        rows_ref[rows, pl.ds(FEATS + STATE, STATE)] = (pr_ref[rows, :] + reads).astype(bf16)


def relay_kernel(*refs):
    pass


def arrange_kernel(in_ref, gi_hbm, gw_hbm, gr_hbm, gw_ref, gr_ref, sems):
    share = gw_ref.shape[0]
    peers = in_ref.shape[0] // share
    copies = []
    for j in range(peers):
        copies.append(
            pltpu.make_async_copy(
                in_ref.at[pl.ds(j * share, share), pl.ds(0, FEATS)],
                gi_hbm.at[:, pl.ds(j * FEATS, FEATS)],
                sems.at[j],
            )
        )
        copies[-1].start()
    for n, (ref, out, at) in enumerate(((gw_ref, gw_hbm, FEATS), (gr_ref, gr_hbm, FEATS + STATE))):
        cols = pl.ds(at, STATE)
        for g in range(GROUPS):
            one, two = pl.ds(2 * g * share, share), pl.ds((2 * g + 1) * share, share)
            ref[:, pl.ds(g * STATE, STATE)] = (
                in_ref[one, cols].astype(f32) + in_ref[two, cols].astype(f32)
            ).astype(bf16)
        copies.append(pltpu.make_async_copy(ref, out, sems.at[peers + n]))
        copies[-1].start()
    for copy in copies:
        copy.wait()


def call(body, outs, ins, scratch=(), flops=0, places=None):
    return pl.pallas_call(
        body,
        out_shape=outs,
        **({} if places is None else {"out_specs": places}),
        in_specs=ins,
        scratch_shapes=scratch,
        compiler_params=pltpu.CompilerParams(vmem_limit_bytes=VMEM_LIMIT),
        cost_estimate=pl.CostEstimate(flops=flops, bytes_accessed=1 << 20, transcendentals=0),
    )


IN_HBM = pl.BlockSpec(memory_space=pltpu.HBM)
IN_ANY = pl.BlockSpec(memory_space=pl.ANY)
IN_VMEM = pl.BlockSpec(memory_space=pltpu.VMEM)
IN_SMEM = pl.BlockSpec(memory_space=pltpu.SMEM)


def per_device(inputs, upstream, step_size, decay_rate, write_proj, read_proj, init_state, skip_gain):
    length = TOKENS_DEV
    wide = pltpu.VMEM((length, FEATS), bf16)
    wide32 = pltpu.VMEM((length, FEATS), f32)
    thin = pltpu.VMEM((length, STATE), bf16)
    thin32 = pltpu.VMEM((length, STATE), f32)
    parts = pltpu.VMEM(((CHUNKS + 1) * STATE, FEATS), f32)
    own, xdh, xdl, xuh, xul, dy, w, r, bt, early, late = call(
        sums_kernel,
        (
            pltpu.VMEM((2 * STATE + 8, FEATS), f32),
            wide, wide, wide, wide, wide, thin, thin,
            pltpu.VMEM((HEADS_DEV, length), f32),
            parts,
            parts,
        ),
        [IN_HBM] * 6,
        [
            pltpu.VMEM((length, FEATS), bf16),
            pltpu.VMEM((HEADS_DEV, length), f32),
            pltpu.VMEM((HEADS_DEV, length), f32),
            pltpu.SMEM((HEADS_DEV,), f32),
            pltpu.SemaphoreType.DMA((CHUNKS + 1, 4)),
        ],
        flops=1 << 30,
    )(
        *(
            pltpu.with_memory_space_constraint(a, pltpu.HBM)
            for a in (inputs, upstream, write_proj, read_proj, step_size.T, decay_rate)
        )
    )

    swap = [(i, i ^ 1) for i in range(2 * CHIPS)]

    def fan(hop):
        up = [(2 * z, 2 * ((z + hop) % CHIPS)) for z in range(CHIPS)]
        down = [(2 * z + 1, 2 * ((z - hop) % CHIPS) + 1) for z in range(CHIPS)]
        return up + down

    other = lax.ppermute(own, "ctx", swap)
    message = jax.ShapeDtypeStruct((ROWS, FEATS), f32)
    messages = call(
        message_kernel,
        (message, message, message, jax.ShapeDtypeStruct((ROWS, FEATS // 2), f32)),
        [IN_VMEM, IN_VMEM],
        [pltpu.VMEM((ROWS, FEATS), f32), pltpu.VMEM((ROWS, FEATS), f32)],
        flops=1 << 20,
    )(own, other)
    mine = [
        lax.ppermute(m.astype(jnp.float16), "ctx", fan(hop))
        for m, hop in zip(messages, (1, 2, 3, FAR))
    ]

    local = call(
        local_kernel,
        (wide32, wide32, thin32, thin32, pltpu.VMEM((STATE, FEATS), f32)),
        [IN_VMEM] * 8 + [IN_SMEM, IN_VMEM],
        flops=0,
    )(xdh, xdl, xuh, xul, dy, w, r, bt, skip_gain, init_state)
    def after(m, token):
        return lax.optimization_barrier((m, token))[0]

    near = mine[:3]
    far = after(mine[3], local[2])
    mine = [after(m, far) for m in near] + [far]
    theirs = [lax.ppermute(m, "ctx", swap).astype(f32) for m in mine]
    mine = [m.astype(f32) for m in mine]

    rows = call(
        finish_kernel,
        jax.ShapeDtypeStruct((length, FEATS + 2 * STATE), bf16),
        [IN_VMEM] * 22,
        [
            pltpu.VMEM((CHUNKS * 2 * STATE, FEATS), bf16),
            pltpu.VMEM((CHUNKS * 2 * STATE, FEATS), bf16),
            pltpu.VMEM((STATE, FEATS), f32),
            pltpu.VMEM((STATE, FEATS), f32),
        ],
        flops=1 << 30,
    )(own, other, *mine, *theirs, xdh, xdl, xuh, xul, w, early, late, *local)

    moved = lax.all_to_all(rows, "head", split_axis=0, concat_axis=0, tiled=True)
    share = length // lax.axis_size("head")
    return call(
        arrange_kernel,
        (
            jax.ShapeDtypeStruct((share, HEADS * HEAD_SIZE), bf16),
            jax.ShapeDtypeStruct((share, GROUPS * STATE), bf16),
            jax.ShapeDtypeStruct((share, GROUPS * STATE), bf16),
        ),
        [IN_VMEM],
        [
            pltpu.VMEM((share, GROUPS * STATE), bf16),
            pltpu.VMEM((share, GROUPS * STATE), bf16),
            pltpu.SemaphoreType.DMA((lax.axis_size("head") + 2,)),
        ],
        places=(IN_HBM,) * 3,
    )(moved)


def solution(mesh):
    placed = (
        P("ctx", "head"),
        P("ctx", "head"),
        P("ctx", "head"),
        P("head"),
        P("ctx", None),
        P("ctx", None),
        P("head", None, None),
        P("head"),
    )
    return jax.shard_map(
        per_device,
        mesh=mesh,
        in_specs=placed,
        out_specs=(P(("ctx", "head"), None), P(("ctx", "head"), None), P(("ctx", "head"), None)),
        check_vma=False,
    )
```

```python
import functools

import jax
import jax.numpy as jnp
from jax import lax
from jax.experimental import pallas as pl
from jax.experimental.pallas import tpu as pltpu
from jax.sharding import PartitionSpec as P

HEADS = 128
HEAD_SIZE = 64
STATE = 128
GROUPS = 8
TOKENS_DEV = 1024
HEADS_DEV = 8
FEATS = HEADS_DEV * HEAD_SIZE
CHUNK = 256
CHUNKS = TOKENS_DEV // CHUNK
CHIPS = 8
FAR = CHIPS // 2
ROWS = STATE + 8
LEAST = 1e-30

f32 = jnp.float32
bf16 = jnp.bfloat16
VMEM_LIMIT = 12 * 1024 * 1024


def nn(a, b):
    return lax.dot_general(a, b, (((1,), (0,)), ((), ())), preferred_element_type=f32)


def nt(a, b):
    return lax.dot_general(a, b, (((1,), (1,)), ((), ())), preferred_element_type=f32)


def tn(a, b):
    return lax.dot_general(a, b, (((0,), (0,)), ((), ())), preferred_element_type=f32)


def halves(x):
    high = x.astype(bf16)
    return high, (x - high.astype(f32)).astype(bf16)


def parts_of(x):
    high = x.astype(bf16).astype(f32)
    mid = (x - high).astype(bf16).astype(f32)
    return [high, mid, x - high - mid]


def head_columns():
    row = lax.broadcasted_iota(jnp.int32, (3 * HEADS_DEV, FEATS), 0) % HEADS_DEV
    col = lax.broadcasted_iota(jnp.int32, (3 * HEADS_DEV, FEATS), 1) // HEAD_SIZE
    return jnp.where(row == col, 1.0, 0.0).astype(bf16)


def spread(per_head, columns):
    high = per_head.astype(bf16).astype(f32)
    rest = per_head - high
    mid = rest.astype(bf16).astype(f32)
    low = rest - mid
    return tn(jnp.concatenate([high, mid, low], axis=0).astype(bf16), columns)


def head_vector(ref):
    row = lax.broadcasted_iota(jnp.int32, (HEADS_DEV, STATE), 0)
    out = jnp.zeros((HEADS_DEV, STATE), f32)
    for h in range(HEADS_DEV):
        out = jnp.where(row == h, ref[h], out)
    return out


def cumulate(x):
    width = 128
    runs = x.shape[1] // width
    stacked = jnp.concatenate([x[:, k * width : (k + 1) * width] for k in range(runs)], axis=0)
    row = lax.broadcasted_iota(jnp.int32, (width, width), 0)
    col = lax.broadcasted_iota(jnp.int32, (width, width), 1)
    ones = jnp.where(row <= col, 1.0, 0.0).astype(bf16)
    parts = jnp.concatenate(parts_of(stacked), axis=1).astype(bf16)
    inner = nn(parts, jnp.concatenate([ones] * 3, axis=0))
    out, offset = [], jnp.zeros((HEADS_DEV, width), f32)
    for k in range(runs):
        run = inner[k * HEADS_DEV : (k + 1) * HEADS_DEV]
        out.append(run + offset)
        offset = offset + jnp.broadcast_to(run[:, width - 1 :], (HEADS_DEV, width))
    return jnp.concatenate(out, axis=1)


def rows_of(i):
    return pl.ds(i * CHUNK if isinstance(i, int) else pl.multiple_of(i * CHUNK, CHUNK), CHUNK)


def slot(i):
    return pl.ds(i * STATE if isinstance(i, int) else pl.multiple_of(i * STATE, STATE), STATE)


def sums_kernel(
    u_hbm, dy_hbm, w_hbm, r_hbm, step_hbm, rate_hbm,
    out_ref, xdh_ref, xdl_ref, xuh_ref, xul_ref, dy_ref, w_ref, r_ref, back_ref, early_ref, late_ref,
    u_ref, ahead_ref, step_ref, rate_ref, sems,
):
    column = pl.multiple_of(lax.axis_index("head") // 2 * STATE, STATE)
    small = [
        pltpu.make_async_copy(step_hbm, step_ref, sems.at[CHUNKS, 0]),
        pltpu.make_async_copy(rate_hbm, rate_ref, sems.at[CHUNKS, 1]),
    ]
    for copy in small:
        copy.start()

    def copies(k):
        rows, back = rows_of(k), rows_of(CHUNKS - 1 - k)
        return [
            pltpu.make_async_copy(u_hbm.at[rows, :], u_ref.at[rows, :], sems.at[k, 0]),
            pltpu.make_async_copy(w_hbm.at[rows, pl.ds(column, STATE)], w_ref.at[rows, :], sems.at[k, 1]),
            pltpu.make_async_copy(dy_hbm.at[back, :], dy_ref.at[back, :], sems.at[k, 2]),
            pltpu.make_async_copy(r_hbm.at[back, pl.ds(column, STATE)], r_ref.at[back, :], sems.at[k, 3]),
        ]

    for k in range(CHUNKS):
        for copy in copies(k):
            copy.start()
    columns = head_columns()
    for copy in small:
        copy.wait()
    steps = step_ref[...]
    rate = head_vector(rate_ref)[:, :1]
    cum = cumulate(-steps * rate)
    last = cum[:, TOKENS_DEV - 1 :]
    middle = 0.5 * last
    ahead = jnp.exp(cum - middle)
    behind = jnp.exp(middle - cum) * steps
    wide = lambda x: spread(jnp.broadcast_to(x, (HEADS_DEV, STATE)), columns)
    half = wide(jnp.exp(middle))
    for i in range(CHUNKS):
        lanes = slice(i * CHUNK, (i + 1) * CHUNK)
        back_ref[rows_of(i), :] = spread(behind[:, lanes], columns)
        ahead_ref[rows_of(i), :] = spread(ahead[:, lanes], columns)
    early_ref[pl.ds(0, STATE), :] = jnp.zeros((STATE, FEATS), f32)
    late_ref[pl.ds(CHUNKS * STATE, STATE), :] = jnp.zeros((STATE, FEATS), f32)

    def weigh(weights, i, values, high_ref, low_ref, vectors):
        rows = rows_of(i)
        high, low = halves(weights[rows, :] * values[rows, :].astype(f32))
        high_ref[rows, :] = high
        low_ref[rows, :] = low
        both = tn(vectors[rows, :], jnp.concatenate([high, low], axis=1))
        return both[:, :FEATS] + both[:, FEATS:]

    def step(k):
        for copy in copies(k):
            copy.wait()
        early_ref[slot(k + 1), :] = early_ref[slot(k), :] + weigh(back_ref, k, u_ref, xuh_ref, xul_ref, w_ref)
        i = CHUNKS - 1 - k
        late_ref[slot(i), :] = late_ref[slot(i + 1), :] + weigh(ahead_ref, i, dy_ref, xdh_ref, xdl_ref, r_ref)

    for k in range(CHUNKS):
        step(k)
    out_ref[pl.ds(0, STATE), :] = half * early_ref[slot(CHUNKS), :]
    out_ref[pl.ds(STATE, STATE), :] = half * late_ref[slot(0), :]
    out_ref[pl.ds(2 * STATE, 8), :] = wide(last)[:8, :]


def message_kernel(own_ref, other_ref, a_ref, b_ref, c_ref, far_ref, w_ref, r_ref):
    place = lax.axis_index("ctx")
    chip, core = place // 2, place % 2
    own_log = own_ref[pl.ds(2 * STATE, 1), :]
    other_log = other_ref[pl.ds(2 * STATE, 1), :]
    own_decay = jnp.exp(own_log)
    other_decay = jnp.exp(other_log)
    first = core == 0
    one = jnp.ones_like(own_decay)
    logs = parts_of(own_log + other_log)
    for ref, left, right, at in (
        (w_ref, jnp.where(first, other_decay, one), jnp.where(first, one, own_decay), 0),
        (r_ref, jnp.where(first, one, other_decay), jnp.where(first, own_decay, one), STATE),
    ):
        rows = pl.ds(at, STATE)
        total = left * own_ref[rows, :] + right * other_ref[rows, :]
        scale = jnp.maximum(jnp.max(jnp.abs(total), axis=0, keepdims=True), LEAST)
        ref[pl.ds(0, STATE), :] = total * (1.0 / scale)
        ref[pl.ds(STATE, 8), :] = jnp.concatenate(
            logs + parts_of(jnp.log(scale)) + [jnp.zeros((2, FEATS), f32)], axis=0
        )
    for hop, ref in ((1, a_ref), (2, b_ref), (3, c_ref)):
        to_later = jnp.where(first, chip + hop < CHIPS, chip - hop < 0)

        @pl.when(to_later)
        def _():
            ref[...] = w_ref[...]

        @pl.when(jnp.logical_not(to_later))
        def _():
            ref[...] = r_ref[...]

    half = FEATS // 2
    later = chip < FAR
    for part in range(2):
        cols = pl.ds(part * half, half)

        @pl.when(jnp.logical_and(later, core == part))
        def _():
            far_ref[...] = w_ref[:, cols]

        @pl.when(jnp.logical_and(jnp.logical_not(later), core == part))
        def _():
            far_ref[...] = r_ref[:, cols]


def local_kernel(
    xdh_ref, xdl_ref, xuh_ref, xul_ref, dy_ref, w_ref, r_ref, back_ref, skip_ref, init_ref,
    gi_ref, pw_ref, pr_ref, init_t_ref,
):
    columns = head_columns()
    skip = spread(head_vector(skip_ref), columns)[:1, :]
    init_t_ref[...] = init_ref[...].reshape(FEATS, STATE).T
    row = lax.broadcasted_iota(jnp.int32, (CHUNK, CHUNK), 0)
    col = lax.broadcasted_iota(jnp.int32, (CHUNK, CHUNK), 1)
    keep = col >= row
    for i in range(CHUNKS):
        rows = rows_of(i)
        writes, reads = w_ref[rows, :], r_ref[rows, :]
        uh, ul = xuh_ref[rows, :], xul_ref[rows, :]
        dh, dl = xdh_ref[rows, :], xdl_ref[rows, :]
        pairs = nt(jnp.concatenate([uh, uh, ul], axis=1), jnp.concatenate([dh, dl, dh], axis=1))
        ph, plow = halves(jnp.where(keep, pairs, 0.0))
        gh, gl = halves(jnp.where(keep, nt(writes, reads), 0.0))
        total = nn(jnp.concatenate([gh, gh, gl], axis=1), jnp.concatenate([dh, dl, dh], axis=0))
        gi_ref[rows, :] = back_ref[rows, :] * total + skip * dy_ref[rows, :].astype(f32)
        pw_ref[rows, :] = nn(ph, reads) + nn(plow, reads)
        pr_ref[rows, :] = tn(ph, writes) + tn(plow, writes)


def finish_kernel(
    own_ref, other_ref, a_ref, b_ref, c_ref, far_ref, oa_ref, ob_ref, oc_ref, ofar_ref,
    xdh_ref, xdl_ref, xuh_ref, xul_ref, w_ref, early_ref, late_ref, back_ref,
    gi_ref, pw_ref, pr_ref, init_t_ref,
    rows_ref, s_ref, t_ref, states_ref, adjoints_ref,
):
    place = lax.axis_index("ctx")
    chip, core = place // 2, place % 2
    first = core == 0
    mine, theirs = (a_ref, b_ref, c_ref), (oa_ref, ob_ref, oc_ref)

    logs_at = pl.ds(STATE, 8)

    def logs(rows):
        return rows[0:1] + rows[1:2] + rows[2:3], rows[3:4] + rows[4:5] + rows[5:6]

    below, above = {}, {}
    for hop in range(1, FAR):
        own_rows, other_rows = mine[hop - 1][logs_at, :], theirs[hop - 1][logs_at, :]
        low, high = jnp.where(first, own_rows, other_rows), jnp.where(first, other_rows, own_rows)
        below[hop] = above[CHIPS - hop] = logs(low)
        above[hop] = below[CHIPS - hop] = logs(high)
    own_rows, other_rows = far_ref[logs_at, :], ofar_ref[logs_at, :]
    below[FAR] = above[FAR] = logs(
        jnp.concatenate(
            [jnp.where(first, own_rows, other_rows), jnp.where(first, other_rows, own_rows)], axis=1
        )
    )

    def weigh(table, inside):
        weights, total = {}, jnp.zeros((1, FEATS), f32)
        for hop in range(1, CHIPS):
            decay, scale = table[hop]
            weights[hop] = jnp.where(inside(hop), jnp.exp(total + scale), 0.0)
            total = total + jnp.where(inside(hop), decay, 0.0)
        return weights, total

    to_state, total = weigh(below, lambda hop: chip - hop >= 0)
    to_adjoint, _ = weigh(above, lambda hop: chip + hop < CHIPS)
    weight_init = jnp.exp(total)
    terms = []
    for hop in range(1, FAR):
        low = to_state[hop], to_adjoint[CHIPS - hop]
        high = to_state[CHIPS - hop], to_adjoint[hop]
        for ref, own in ((mine[hop - 1], True), (theirs[hop - 1], False)):
            one, two = (low, high) if own else (high, low)
            terms.append((ref, jnp.where(first, one[0], two[0]), jnp.where(first, one[1], two[1])))

    own_log = own_ref[pl.ds(2 * STATE, 1), :]
    other_decay = jnp.exp(other_ref[pl.ds(2 * STATE, 1), :])
    half = jnp.exp(0.5 * own_log)
    keep_s = jnp.where(first, half, half * other_decay)
    keep_a = jnp.where(first, half * other_decay, half)
    add_s = jnp.where(first, 0.0, half)
    add_a = jnp.where(first, half, 0.0)
    step = 32
    for at in range(0, STATE, step):
        rows = pl.ds(at, step)
        near, distant = far_ref[rows, :], ofar_ref[rows, :]
        middle = jnp.concatenate(
            [jnp.where(first, near, distant), jnp.where(first, distant, near)], axis=1
        )
        state = weight_init * init_t_ref[rows, :] + to_state[FAR] * middle
        adjoint = to_adjoint[FAR] * middle
        for ref, for_state, for_adjoint in terms:
            value = ref[rows, :]
            state = state + for_state * value
            adjoint = adjoint + for_adjoint * value
        states_ref[rows, :] = keep_s * state + add_s * other_ref[rows, :]
        adjoints_ref[rows, :] = keep_a * adjoint + add_a * other_ref[pl.ds(STATE + at, step), :]

    for i in range(CHUNKS):
        rows = rows_of(i)
        base = i * 2 * STATE
        state = states_ref[...] + early_ref[slot(i), :]
        adjoint = adjoints_ref[...] + late_ref[slot(i + 1), :]
        sh, sl = halves(state)
        th, tl = halves(adjoint)
        s_ref[pl.ds(base, STATE), :] = sh
        s_ref[pl.ds(base + STATE, STATE), :] = sl
        t_ref[pl.ds(base, STATE), :] = th
        t_ref[pl.ds(base + STATE, STATE), :] = tl
        both, high = pl.ds(base, 2 * STATE), pl.ds(base, STATE)
        reads = nt(xdh_ref[rows, :], s_ref[both, :])
        reads = reads[:, :STATE] + reads[:, STATE:] + nt(xdl_ref[rows, :], s_ref[high, :])
        writes = nt(xuh_ref[rows, :], t_ref[both, :])
        writes = writes[:, :STATE] + writes[:, STATE:] + nt(xul_ref[rows, :], t_ref[high, :])
        vectors = w_ref[rows, :]
        through = nn(jnp.concatenate([vectors, vectors], axis=1), t_ref[both, :])
        rows_ref[rows, pl.ds(0, FEATS)] = (gi_ref[rows, :] + back_ref[rows, :] * through).astype(bf16)
        rows_ref[rows, pl.ds(FEATS, STATE)] = (pw_ref[rows, :] + writes).astype(bf16)
        rows_ref[rows, pl.ds(FEATS + STATE, STATE)] = (pr_ref[rows, :] + reads).astype(bf16)


def relay_kernel(*refs):
    pass


def arrange_kernel(in_ref, gi_hbm, gw_hbm, gr_hbm, gw_ref, gr_ref, sems):
    share = gw_ref.shape[0]
    peers = in_ref.shape[0] // share
    copies = []
    for j in range(peers):
        copies.append(
            pltpu.make_async_copy(
                in_ref.at[pl.ds(j * share, share), pl.ds(0, FEATS)],
                gi_hbm.at[:, pl.ds(j * FEATS, FEATS)],
                sems.at[j],
            )
        )
        copies[-1].start()
    for n, (ref, out, at) in enumerate(((gw_ref, gw_hbm, FEATS), (gr_ref, gr_hbm, FEATS + STATE))):
        cols = pl.ds(at, STATE)
        for g in range(GROUPS):
            one, two = pl.ds(2 * g * share, share), pl.ds((2 * g + 1) * share, share)
            ref[:, pl.ds(g * STATE, STATE)] = (
                in_ref[one, cols].astype(f32) + in_ref[two, cols].astype(f32)
            ).astype(bf16)
        copies.append(pltpu.make_async_copy(ref, out, sems.at[peers + n]))
        copies[-1].start()
    for copy in copies:
        copy.wait()


def call(body, outs, ins, scratch=(), flops=0, places=None):
    return pl.pallas_call(
        body,
        out_shape=outs,
        **({} if places is None else {"out_specs": places}),
        in_specs=ins,
        scratch_shapes=scratch,
        compiler_params=pltpu.CompilerParams(vmem_limit_bytes=VMEM_LIMIT),
        cost_estimate=pl.CostEstimate(flops=flops, bytes_accessed=1 << 20, transcendentals=0),
    )


IN_HBM = pl.BlockSpec(memory_space=pltpu.HBM)
IN_ANY = pl.BlockSpec(memory_space=pl.ANY)
IN_VMEM = pl.BlockSpec(memory_space=pltpu.VMEM)
IN_SMEM = pl.BlockSpec(memory_space=pltpu.SMEM)


def per_device(inputs, upstream, step_size, decay_rate, write_proj, read_proj, init_state, skip_gain):
    length = TOKENS_DEV
    wide = pltpu.VMEM((length, FEATS), bf16)
    wide32 = pltpu.VMEM((length, FEATS), f32)
    thin = pltpu.VMEM((length, STATE), bf16)
    thin32 = pltpu.VMEM((length, STATE), f32)
    parts = pltpu.VMEM(((CHUNKS + 1) * STATE, FEATS), f32)
    own, xdh, xdl, xuh, xul, dy, w, r, back, early, late = call(
        sums_kernel,
        (
            pltpu.VMEM((2 * STATE + 8, FEATS), f32),
            wide, wide, wide, wide, wide, thin, thin,
            wide32,
            parts,
            parts,
        ),
        [IN_HBM] * 6,
        [
            pltpu.VMEM((length, FEATS), bf16),
            pltpu.VMEM((length, FEATS), f32),
            pltpu.VMEM((HEADS_DEV, length), f32),
            pltpu.SMEM((HEADS_DEV,), f32),
            pltpu.SemaphoreType.DMA((CHUNKS + 1, 4)),
        ],
        flops=1 << 30,
    )(
        *(
            pltpu.with_memory_space_constraint(a, pltpu.HBM)
            for a in (inputs, upstream, write_proj, read_proj, step_size.T, decay_rate)
        )
    )

    swap = [(i, i ^ 1) for i in range(2 * CHIPS)]

    def fan(hop):
        up = [(2 * z, 2 * ((z + hop) % CHIPS)) for z in range(CHIPS)]
        down = [(2 * z + 1, 2 * ((z - hop) % CHIPS) + 1) for z in range(CHIPS)]
        return up + down

    other = lax.ppermute(own, "ctx", swap)
    message = jax.ShapeDtypeStruct((ROWS, FEATS), f32)
    messages = call(
        message_kernel,
        (message, message, message, jax.ShapeDtypeStruct((ROWS, FEATS // 2), f32)),
        [IN_VMEM, IN_VMEM],
        [pltpu.VMEM((ROWS, FEATS), f32), pltpu.VMEM((ROWS, FEATS), f32)],
        flops=1 << 20,
    )(own, other)
    mine = [
        lax.ppermute(m.astype(jnp.float16), "ctx", fan(hop))
        for m, hop in zip(messages, (1, 2, 3, FAR))
    ]

    local = call(
        local_kernel,
        (wide32, thin32, thin32, pltpu.VMEM((STATE, FEATS), f32)),
        [IN_VMEM] * 8 + [IN_SMEM, IN_VMEM],
        flops=0,
    )(xdh, xdl, xuh, xul, dy, w, r, back, skip_gain, init_state)
    def after(m, token):
        return lax.optimization_barrier((m, token))[0]

    lead = after(mine[1], local[1])
    mine = [lead if n == 1 else after(m, lead) for n, m in enumerate(mine)]
    theirs = [lax.ppermute(m, "ctx", swap).astype(f32) for m in mine]
    mine = [m.astype(f32) for m in mine]

    rows = call(
        finish_kernel,
        jax.ShapeDtypeStruct((length, FEATS + 2 * STATE), bf16),
        [IN_VMEM] * 22,
        [
            pltpu.VMEM((CHUNKS * 2 * STATE, FEATS), bf16),
            pltpu.VMEM((CHUNKS * 2 * STATE, FEATS), bf16),
            pltpu.VMEM((STATE, FEATS), f32),
            pltpu.VMEM((STATE, FEATS), f32),
        ],
        flops=1 << 30,
    )(own, other, *mine, *theirs, xdh, xdl, xuh, xul, w, early, late, back, *local)

    moved = lax.all_to_all(rows, "head", split_axis=0, concat_axis=0, tiled=True)
    share = length // lax.axis_size("head")
    return call(
        arrange_kernel,
        (
            jax.ShapeDtypeStruct((share, HEADS * HEAD_SIZE), bf16),
            jax.ShapeDtypeStruct((share, GROUPS * STATE), bf16),
            jax.ShapeDtypeStruct((share, GROUPS * STATE), bf16),
        ),
        [IN_VMEM],
        [
            pltpu.VMEM((share, GROUPS * STATE), bf16),
            pltpu.VMEM((share, GROUPS * STATE), bf16),
            pltpu.SemaphoreType.DMA((lax.axis_size("head") + 2,)),
        ],
        places=(IN_HBM,) * 3,
    )(moved)


def solution(mesh):
    placed = (
        P("ctx", "head"),
        P("ctx", "head"),
        P("ctx", "head"),
        P("head"),
        P("ctx", None),
        P("ctx", None),
        P("head", None, None),
        P("head"),
    )
    return jax.shard_map(
        per_device,
        mesh=mesh,
        in_specs=placed,
        out_specs=(P(("ctx", "head"), None), P(("ctx", "head"), None), P(("ctx", "head"), None)),
        check_vma=False,
    )
```

```python
import functools

import jax
import jax.numpy as jnp
from jax import lax
from jax.experimental import pallas as pl
from jax.experimental.pallas import tpu as pltpu
from jax.sharding import PartitionSpec as P

HEADS = 128
HEAD_SIZE = 64
STATE = 128
GROUPS = 8
TOKENS_DEV = 1024
HEADS_DEV = 8
FEATS = HEADS_DEV * HEAD_SIZE
CHUNK = 256
CHUNKS = TOKENS_DEV // CHUNK
CHIPS = 8
FAR = CHIPS // 2
ROWS = STATE + 8
LEAST = 1e-30

f32 = jnp.float32
bf16 = jnp.bfloat16
VMEM_LIMIT = 12 * 1024 * 1024


def nn(a, b):
    return lax.dot_general(a, b, (((1,), (0,)), ((), ())), preferred_element_type=f32)


def nt(a, b):
    return lax.dot_general(a, b, (((1,), (1,)), ((), ())), preferred_element_type=f32)


def tn(a, b):
    return lax.dot_general(a, b, (((0,), (0,)), ((), ())), preferred_element_type=f32)


def halves(x):
    high = x.astype(bf16)
    return high, (x - high.astype(f32)).astype(bf16)


def parts_of(x):
    high = x.astype(bf16).astype(f32)
    mid = (x - high).astype(bf16).astype(f32)
    return [high, mid, x - high - mid]


def head_columns():
    row = lax.broadcasted_iota(jnp.int32, (3 * HEADS_DEV, FEATS), 0) % HEADS_DEV
    col = lax.broadcasted_iota(jnp.int32, (3 * HEADS_DEV, FEATS), 1) // HEAD_SIZE
    return jnp.where(row == col, 1.0, 0.0).astype(bf16)


def spread(per_head, columns):
    high = per_head.astype(bf16).astype(f32)
    rest = per_head - high
    mid = rest.astype(bf16).astype(f32)
    low = rest - mid
    return tn(jnp.concatenate([high, mid, low], axis=0).astype(bf16), columns)


def head_vector(ref):
    row = lax.broadcasted_iota(jnp.int32, (HEADS_DEV, STATE), 0)
    out = jnp.zeros((HEADS_DEV, STATE), f32)
    for h in range(HEADS_DEV):
        out = jnp.where(row == h, ref[h], out)
    return out


def cumulate(x):
    width = 128
    runs = x.shape[1] // width
    stacked = jnp.concatenate([x[:, k * width : (k + 1) * width] for k in range(runs)], axis=0)
    row = lax.broadcasted_iota(jnp.int32, (width, width), 0)
    col = lax.broadcasted_iota(jnp.int32, (width, width), 1)
    ones = jnp.where(row <= col, 1.0, 0.0).astype(bf16)
    parts = jnp.concatenate(parts_of(stacked), axis=1).astype(bf16)
    inner = nn(parts, jnp.concatenate([ones] * 3, axis=0))
    out, offset = [], jnp.zeros((HEADS_DEV, width), f32)
    for k in range(runs):
        run = inner[k * HEADS_DEV : (k + 1) * HEADS_DEV]
        out.append(run + offset)
        offset = offset + jnp.broadcast_to(run[:, width - 1 :], (HEADS_DEV, width))
    return jnp.concatenate(out, axis=1)


def rows_of(i):
    return pl.ds(i * CHUNK if isinstance(i, int) else pl.multiple_of(i * CHUNK, CHUNK), CHUNK)


def slot(i):
    return pl.ds(i * STATE if isinstance(i, int) else pl.multiple_of(i * STATE, STATE), STATE)


def sums_kernel(
    u_hbm, dy_hbm, w_hbm, r_hbm, step_hbm, rate_hbm,
    out_ref, xdh_ref, xdl_ref, xuh_ref, xul_ref, dy_ref, w_ref, r_ref, back_ref, early_ref, late_ref,
    u_ref, ahead_ref, step_ref, rate_ref, sems,
):
    column = pl.multiple_of(lax.axis_index("head") // 2 * STATE, STATE)
    small = [
        pltpu.make_async_copy(step_hbm, step_ref, sems.at[CHUNKS, 0]),
        pltpu.make_async_copy(rate_hbm, rate_ref, sems.at[CHUNKS, 1]),
    ]
    for copy in small:
        copy.start()

    def copies(k):
        rows, back = rows_of(k), rows_of(CHUNKS - 1 - k)
        return [
            pltpu.make_async_copy(u_hbm.at[rows, :], u_ref.at[rows, :], sems.at[k, 0]),
            pltpu.make_async_copy(w_hbm.at[rows, pl.ds(column, STATE)], w_ref.at[rows, :], sems.at[k, 1]),
            pltpu.make_async_copy(dy_hbm.at[back, :], dy_ref.at[back, :], sems.at[k, 2]),
            pltpu.make_async_copy(r_hbm.at[back, pl.ds(column, STATE)], r_ref.at[back, :], sems.at[k, 3]),
        ]

    for k in range(CHUNKS):
        for copy in copies(k):
            copy.start()
    columns = head_columns()
    for copy in small:
        copy.wait()
    steps = step_ref[...]
    rate = head_vector(rate_ref)[:, :1]
    cum = cumulate(-steps * rate)
    last = cum[:, TOKENS_DEV - 1 :]
    middle = 0.5 * last
    ahead = jnp.exp(cum - middle)
    behind = jnp.exp(middle - cum) * steps
    wide = lambda x: spread(jnp.broadcast_to(x, (HEADS_DEV, STATE)), columns)
    half = wide(jnp.exp(middle))
    for i in range(CHUNKS):
        lanes = slice(i * CHUNK, (i + 1) * CHUNK)
        back_ref[rows_of(i), :] = spread(behind[:, lanes], columns)
        ahead_ref[rows_of(i), :] = spread(ahead[:, lanes], columns)
    early_ref[pl.ds(0, STATE), :] = jnp.zeros((STATE, FEATS), f32)
    late_ref[pl.ds(CHUNKS * STATE, STATE), :] = jnp.zeros((STATE, FEATS), f32)

    def weigh(weights, i, values, high_ref, low_ref, vectors):
        rows = rows_of(i)
        high, low = halves(weights[rows, :] * values[rows, :].astype(f32))
        high_ref[rows, :] = high
        low_ref[rows, :] = low
        both = tn(vectors[rows, :], jnp.concatenate([high, low], axis=1))
        return both[:, :FEATS] + both[:, FEATS:]

    def step(k):
        for copy in copies(k):
            copy.wait()
        early_ref[slot(k + 1), :] = early_ref[slot(k), :] + weigh(back_ref, k, u_ref, xuh_ref, xul_ref, w_ref)
        i = CHUNKS - 1 - k
        late_ref[slot(i), :] = late_ref[slot(i + 1), :] + weigh(ahead_ref, i, dy_ref, xdh_ref, xdl_ref, r_ref)

    for k in range(CHUNKS):
        step(k)
    out_ref[pl.ds(0, STATE), :] = half * early_ref[slot(CHUNKS), :]
    out_ref[pl.ds(STATE, STATE), :] = half * late_ref[slot(0), :]
    out_ref[pl.ds(2 * STATE, 8), :] = wide(last)[:8, :]


def message_kernel(own_ref, other_ref, a_ref, b_ref, c_ref, far_ref, w_ref, r_ref):
    place = lax.axis_index("ctx")
    chip, core = place // 2, place % 2
    own_log = own_ref[pl.ds(2 * STATE, 1), :]
    other_log = other_ref[pl.ds(2 * STATE, 1), :]
    own_decay = jnp.exp(own_log)
    other_decay = jnp.exp(other_log)
    first = core == 0
    one = jnp.ones_like(own_decay)
    logs = parts_of(own_log + other_log)
    for ref, left, right, at in (
        (w_ref, jnp.where(first, other_decay, one), jnp.where(first, one, own_decay), 0),
        (r_ref, jnp.where(first, one, other_decay), jnp.where(first, own_decay, one), STATE),
    ):
        rows = pl.ds(at, STATE)
        total = left * own_ref[rows, :] + right * other_ref[rows, :]
        scale = jnp.maximum(jnp.max(jnp.abs(total), axis=0, keepdims=True), LEAST)
        ref[pl.ds(0, STATE), :] = total * (1.0 / scale)
        ref[pl.ds(STATE, 8), :] = jnp.concatenate(
            logs + parts_of(jnp.log(scale)) + [jnp.zeros((2, FEATS), f32)], axis=0
        )
    for hop, ref in ((1, a_ref), (2, b_ref), (3, c_ref)):
        to_later = jnp.where(first, chip + hop < CHIPS, chip - hop < 0)

        @pl.when(to_later)
        def _():
            ref[...] = w_ref[...]

        @pl.when(jnp.logical_not(to_later))
        def _():
            ref[...] = r_ref[...]

    half = FEATS // 2
    later = chip < FAR
    for part in range(2):
        cols = pl.ds(part * half, half)

        @pl.when(jnp.logical_and(later, core == part))
        def _():
            far_ref[...] = w_ref[:, cols]

        @pl.when(jnp.logical_and(jnp.logical_not(later), core == part))
        def _():
            far_ref[...] = r_ref[:, cols]


def local_kernel(
    xdh_ref, xdl_ref, xuh_ref, xul_ref, dy_ref, w_ref, r_ref, back_ref, skip_ref, init_ref,
    gi_ref, pw_ref, pr_ref, init_t_ref,
):
    columns = head_columns()
    skip = spread(head_vector(skip_ref), columns)[:1, :]
    init_t_ref[...] = init_ref[...].reshape(FEATS, STATE).T
    row = lax.broadcasted_iota(jnp.int32, (CHUNK, CHUNK), 0)
    col = lax.broadcasted_iota(jnp.int32, (CHUNK, CHUNK), 1)
    keep = col >= row
    for i in range(CHUNKS):
        rows = rows_of(i)
        writes, reads = w_ref[rows, :], r_ref[rows, :]
        uh, ul = xuh_ref[rows, :], xul_ref[rows, :]
        dh, dl = xdh_ref[rows, :], xdl_ref[rows, :]
        pairs = nt(jnp.concatenate([uh, uh, ul], axis=1), jnp.concatenate([dh, dl, dh], axis=1))
        ph, plow = halves(jnp.where(keep, pairs, 0.0))
        gh, gl = halves(jnp.where(keep, nt(writes, reads), 0.0))
        total = nn(jnp.concatenate([gh, gh, gl], axis=1), jnp.concatenate([dh, dl, dh], axis=0))
        gi_ref[rows, :] = back_ref[rows, :] * total + skip * dy_ref[rows, :].astype(f32)
        pw_ref[rows, :] = nn(ph, reads) + nn(plow, reads)
        pr_ref[rows, :] = tn(ph, writes) + tn(plow, writes)


def finish_kernel(
    own_ref, other_ref, a_ref, b_ref, c_ref, far_ref, oa_ref, ob_ref, oc_ref, ofar_ref,
    xdh_ref, xdl_ref, xuh_ref, xul_ref, w_ref, early_ref, late_ref, back_ref,
    gi_ref, pw_ref, pr_ref, init_t_ref,
    rows_ref, s_ref, t_ref, states_ref, adjoints_ref,
):
    place = lax.axis_index("ctx")
    chip, core = place // 2, place % 2
    first = core == 0
    mine, theirs = (a_ref, b_ref, c_ref), (oa_ref, ob_ref, oc_ref)

    logs_at = pl.ds(STATE, 8)

    def logs(rows):
        return rows[0:1] + rows[1:2] + rows[2:3], rows[3:4] + rows[4:5] + rows[5:6]

    below, above = {}, {}
    for hop in range(1, FAR):
        own_rows, other_rows = mine[hop - 1][logs_at, :], theirs[hop - 1][logs_at, :]
        low, high = jnp.where(first, own_rows, other_rows), jnp.where(first, other_rows, own_rows)
        below[hop] = above[CHIPS - hop] = logs(low)
        above[hop] = below[CHIPS - hop] = logs(high)
    own_rows, other_rows = far_ref[logs_at, :], ofar_ref[logs_at, :]
    below[FAR] = above[FAR] = logs(
        jnp.concatenate(
            [jnp.where(first, own_rows, other_rows), jnp.where(first, other_rows, own_rows)], axis=1
        )
    )

    def weigh(table, inside):
        weights, total = {}, jnp.zeros((1, FEATS), f32)
        for hop in range(1, CHIPS):
            decay, scale = table[hop]
            weights[hop] = jnp.where(inside(hop), jnp.exp(total + scale), 0.0)
            total = total + jnp.where(inside(hop), decay, 0.0)
        return weights, total

    to_state, total = weigh(below, lambda hop: chip - hop >= 0)
    to_adjoint, _ = weigh(above, lambda hop: chip + hop < CHIPS)
    weight_init = jnp.exp(total)
    terms = []
    for hop in range(1, FAR):
        low = to_state[hop], to_adjoint[CHIPS - hop]
        high = to_state[CHIPS - hop], to_adjoint[hop]
        for ref, own in ((mine[hop - 1], True), (theirs[hop - 1], False)):
            one, two = (low, high) if own else (high, low)
            terms.append((ref, jnp.where(first, one[0], two[0]), jnp.where(first, one[1], two[1])))

    own_log = own_ref[pl.ds(2 * STATE, 1), :]
    other_decay = jnp.exp(other_ref[pl.ds(2 * STATE, 1), :])
    half = jnp.exp(0.5 * own_log)
    keep_s = jnp.where(first, half, half * other_decay)
    keep_a = jnp.where(first, half * other_decay, half)
    add_s = jnp.where(first, 0.0, half)
    add_a = jnp.where(first, half, 0.0)
    step = 32
    for at in range(0, STATE, step):
        rows = pl.ds(at, step)
        near, distant = far_ref[rows, :], ofar_ref[rows, :]
        middle = jnp.concatenate(
            [jnp.where(first, near, distant), jnp.where(first, distant, near)], axis=1
        )
        state = weight_init * init_t_ref[rows, :] + to_state[FAR] * middle
        adjoint = to_adjoint[FAR] * middle
        for ref, for_state, for_adjoint in terms:
            value = ref[rows, :]
            state = state + for_state * value
            adjoint = adjoint + for_adjoint * value
        states_ref[rows, :] = keep_s * state + add_s * other_ref[rows, :]
        adjoints_ref[rows, :] = keep_a * adjoint + add_a * other_ref[pl.ds(STATE + at, step), :]

    for i in range(CHUNKS):
        rows = rows_of(i)
        base = i * 2 * STATE
        state = states_ref[...] + early_ref[slot(i), :]
        adjoint = adjoints_ref[...] + late_ref[slot(i + 1), :]
        sh, sl = halves(state)
        th, tl = halves(adjoint)
        s_ref[pl.ds(base, STATE), :] = sh
        s_ref[pl.ds(base + STATE, STATE), :] = sl
        t_ref[pl.ds(base, STATE), :] = th
        t_ref[pl.ds(base + STATE, STATE), :] = tl
        both, high = pl.ds(base, 2 * STATE), pl.ds(base, STATE)
        reads = nt(xdh_ref[rows, :], s_ref[both, :])
        reads = reads[:, :STATE] + reads[:, STATE:] + nt(xdl_ref[rows, :], s_ref[high, :])
        writes = nt(xuh_ref[rows, :], t_ref[both, :])
        writes = writes[:, :STATE] + writes[:, STATE:] + nt(xul_ref[rows, :], t_ref[high, :])
        vectors = w_ref[rows, :]
        through = nn(jnp.concatenate([vectors, vectors], axis=1), t_ref[both, :])
        rows_ref[rows, pl.ds(0, FEATS)] = (gi_ref[rows, :] + back_ref[rows, :] * through).astype(bf16)
        rows_ref[rows, pl.ds(FEATS, STATE)] = (pw_ref[rows, :] + writes).astype(bf16)
        rows_ref[rows, pl.ds(FEATS + STATE, STATE)] = (pr_ref[rows, :] + reads).astype(bf16)


def relay_kernel(*refs):
    pass


def arrange_kernel(in_ref, gi_hbm, gw_hbm, gr_hbm, gw_ref, gr_ref, sems):
    share = gw_ref.shape[0]
    peers = in_ref.shape[0] // share
    copies = []
    for j in range(peers):
        copies.append(
            pltpu.make_async_copy(
                in_ref.at[pl.ds(j * share, share), pl.ds(0, FEATS)],
                gi_hbm.at[:, pl.ds(j * FEATS, FEATS)],
                sems.at[j],
            )
        )
        copies[-1].start()
    for n, (ref, out, at) in enumerate(((gw_ref, gw_hbm, FEATS), (gr_ref, gr_hbm, FEATS + STATE))):
        cols = pl.ds(at, STATE)
        for g in range(GROUPS):
            one, two = pl.ds(2 * g * share, share), pl.ds((2 * g + 1) * share, share)
            ref[:, pl.ds(g * STATE, STATE)] = (
                in_ref[one, cols].astype(f32) + in_ref[two, cols].astype(f32)
            ).astype(bf16)
        copies.append(pltpu.make_async_copy(ref, out, sems.at[peers + n]))
        copies[-1].start()
    for copy in copies:
        copy.wait()


def call(body, outs, ins, scratch=(), flops=0, places=None):
    return pl.pallas_call(
        body,
        out_shape=outs,
        **({} if places is None else {"out_specs": places}),
        in_specs=ins,
        scratch_shapes=scratch,
        compiler_params=pltpu.CompilerParams(vmem_limit_bytes=VMEM_LIMIT),
        cost_estimate=pl.CostEstimate(flops=flops, bytes_accessed=1 << 20, transcendentals=0),
    )


IN_HBM = pl.BlockSpec(memory_space=pltpu.HBM)
IN_ANY = pl.BlockSpec(memory_space=pl.ANY)
IN_VMEM = pl.BlockSpec(memory_space=pltpu.VMEM)
IN_SMEM = pl.BlockSpec(memory_space=pltpu.SMEM)


def per_device(inputs, upstream, step_size, decay_rate, write_proj, read_proj, init_state, skip_gain):
    length = TOKENS_DEV
    wide = pltpu.VMEM((length, FEATS), bf16)
    wide32 = pltpu.VMEM((length, FEATS), f32)
    thin = pltpu.VMEM((length, STATE), bf16)
    thin32 = pltpu.VMEM((length, STATE), f32)
    parts = pltpu.VMEM(((CHUNKS + 1) * STATE, FEATS), f32)
    own, xdh, xdl, xuh, xul, dy, w, r, back, early, late = call(
        sums_kernel,
        (
            pltpu.VMEM((2 * STATE + 8, FEATS), f32),
            wide, wide, wide, wide, wide, thin, thin,
            wide32,
            parts,
            parts,
        ),
        [IN_HBM] * 6,
        [
            pltpu.VMEM((length, FEATS), bf16),
            pltpu.VMEM((length, FEATS), f32),
            pltpu.VMEM((HEADS_DEV, length), f32),
            pltpu.SMEM((HEADS_DEV,), f32),
            pltpu.SemaphoreType.DMA((CHUNKS + 1, 4)),
        ],
        flops=1 << 30,
    )(
        *(
            pltpu.with_memory_space_constraint(a, pltpu.HBM)
            for a in (inputs, upstream, write_proj, read_proj, step_size.T, decay_rate)
        )
    )

    swap = [(i, i ^ 1) for i in range(2 * CHIPS)]

    def fan(hop):
        up = [(2 * z, 2 * ((z + hop) % CHIPS)) for z in range(CHIPS)]
        down = [(2 * z + 1, 2 * ((z - hop) % CHIPS) + 1) for z in range(CHIPS)]
        return up + down

    other = lax.ppermute(own, "ctx", swap)
    message = jax.ShapeDtypeStruct((ROWS, FEATS), f32)
    messages = call(
        message_kernel,
        (message, message, message, jax.ShapeDtypeStruct((ROWS, FEATS // 2), f32)),
        [IN_VMEM, IN_VMEM],
        [pltpu.VMEM((ROWS, FEATS), f32), pltpu.VMEM((ROWS, FEATS), f32)],
        flops=1 << 20,
    )(own, other)
    mine = [
        lax.ppermute(m.astype(jnp.float16), "ctx", fan(hop))
        for m, hop in zip(messages, (1, 2, 3, FAR))
    ]

    def after(m, token):
        return lax.optimization_barrier((m, token))[0]

    local = call(
        local_kernel,
        (wide32, thin32, thin32, pltpu.VMEM((STATE, FEATS), f32)),
        [IN_VMEM] * 8 + [IN_SMEM, IN_VMEM],
        flops=0,
    )(xdh, xdl, xuh, xul, dy, w, r, after(back, mine[0]), skip_gain, init_state)
    mine = [mine[0]] + [after(m, local[1]) for m in mine[1:]]
    theirs = [lax.ppermute(m, "ctx", swap).astype(f32) for m in mine]
    mine = [m.astype(f32) for m in mine]

    rows = call(
        finish_kernel,
        jax.ShapeDtypeStruct((length, FEATS + 2 * STATE), bf16),
        [IN_VMEM] * 22,
        [
            pltpu.VMEM((CHUNKS * 2 * STATE, FEATS), bf16),
            pltpu.VMEM((CHUNKS * 2 * STATE, FEATS), bf16),
            pltpu.VMEM((STATE, FEATS), f32),
            pltpu.VMEM((STATE, FEATS), f32),
        ],
        flops=1 << 30,
    )(own, other, *mine, *theirs, xdh, xdl, xuh, xul, w, early, late, back, *local)

    moved = lax.all_to_all(rows, "head", split_axis=0, concat_axis=0, tiled=True)
    share = length // lax.axis_size("head")
    return call(
        arrange_kernel,
        (
            jax.ShapeDtypeStruct((share, HEADS * HEAD_SIZE), bf16),
            jax.ShapeDtypeStruct((share, GROUPS * STATE), bf16),
            jax.ShapeDtypeStruct((share, GROUPS * STATE), bf16),
        ),
        [IN_VMEM],
        [
            pltpu.VMEM((share, GROUPS * STATE), bf16),
            pltpu.VMEM((share, GROUPS * STATE), bf16),
            pltpu.SemaphoreType.DMA((lax.axis_size("head") + 2,)),
        ],
        places=(IN_HBM,) * 3,
    )(moved)


def solution(mesh):
    placed = (
        P("ctx", "head"),
        P("ctx", "head"),
        P("ctx", "head"),
        P("head"),
        P("ctx", None),
        P("ctx", None),
        P("head", None, None),
        P("head"),
    )
    return jax.shard_map(
        per_device,
        mesh=mesh,
        in_specs=placed,
        out_specs=(P(("ctx", "head"), None), P(("ctx", "head"), None), P(("ctx", "head"), None)),
        check_vma=False,
    )
```
